512 devices in a mesh: det: 4 (over y_lo, core), tm: 128 (over z, x, y_hi).
Axes of the slice: x: 4, y: 8 (y_hi: 4, y_lo: 2; y = y_hi * 2 + y_lo), z: 8, core: 2. Of those that a mesh axis runs over, the one named last changes fastest.
Arguments:
- spectra: bfloat16 [4, 256, 32, 2, 128], P('det', 'tm'), may hold values from -200 to 200
- valid: int32 [256], P('tm'), may hold values 0 or 1
- lags: float32 [49152], replicated, may hold values from -0.01 to 0.01
- drift: float32 [49152], replicated, may hold values from -4 to 4
- block_table: int32 [1024, 2], replicated, may hold values from 0 to 95, as said below
Outputs:
- sky_map: float32 [49152], P(('det', 'tm'))
The draws below stay inside these ranges and needn't reach their ends.
Inputs may be any that keep to these rules, and one draw needn't show every extreme that they name: `block_table`: row (2 i + h) * 4 + k, for 0 <= i < 128, h in 0, 1 and 0 <= k < 4, holds a band from h * 32 to h * 32 + 31 and a tile below 96; each aligned block of 2 rows starting at a multiple of 2 has one band, and the 2 bands of one (i, h) are distinct.
All inputs are finite; a program needn't handle non-finite values. No bound on the sum of `valid` on one device may be relied on, other than what follows from the above.
Results may differ from the reference program's by a relative error of at most 0.0037.
Values may be sent and summed in bfloat16 or wider, within the bound.
A program may use at most 64 MiB of HBM per device.

```python
import math
import jax
import jax.numpy as jnp
from jax import lax

F = 8192
P_SIZE = 49152
BW = 128
PT = 512
TPB = 2
BLK_DEV = 4
NBH = 32
NBAND = 64
NTILE = 96
SEGS = 256
NBLK = 1024
BAND_DEV = 2
N_TM = 128


def draw_spectra(key, part):
    noise_key = jax.random.fold_in(key, 0)
    shape = (4, SEGS, NBH, 2, BW)
    bin_half = jnp.arange(4, dtype=jnp.int32) % 2
    position = (bin_half[:, None, None] * (NBH * BW) + jnp.arange(NBH, dtype=jnp.int32)[None, :, None] * BW + jnp.arange(BW, dtype=jnp.int32)[None, None, :]).astype(jnp.float32) / F
    envelope = jnp.power(3.0, 1.0 - position)
    noise_values = jax.random.normal(noise_key, shape, jnp.float32)
    result = noise_values * envelope[:, None, :, None, :]
    return result.astype(jnp.bfloat16)


def pick_bands(band_key):
    return jax.random.permutation(band_key, NBH)[:BAND_DEV]


def draw_block_table(key, part):
    band_key, tile_key = jax.random.split(jax.random.fold_in(key, 7))
    groups = N_TM * 2
    picked = jax.vmap(pick_bands)(jax.random.split(band_key, groups)).astype(jnp.int32)
    offsets = jnp.arange(groups, dtype=jnp.int32) % 2 * NBH
    bands = jnp.repeat(picked + offsets[:, None], TPB, axis=1)
    tile_ids = jax.random.randint(tile_key, (groups, BLK_DEV), 0, NTILE, dtype=jnp.int32)
    return jnp.stack([bands, tile_ids], -1).reshape(NBLK, 2).astype(jnp.int32)


def plant(drawn, key, least, high):
    extent = drawn.shape
    index_at = [jax.random.randint(jax.random.fold_in(key, axis), (), 0, extent[axis]) for axis in range(len(extent))]
    drawn = drawn.at[tuple(index_at)].set(least)
    longest = extent.index(max(extent))
    index_at[longest] = (index_at[longest] + 1) % extent[longest]
    return drawn.at[tuple(index_at)].set(high)


def setup_inputs(seed: int = 0) -> dict:
    key_of = jax.random.split(jax.random.key(seed), 6)
    spectra = draw_spectra(jax.random.fold_in(key_of[5], 71), 0)
    valid = plant((jax.random.randint(key_of[1], (SEGS,), 0, 4) < 3).astype(jnp.int32), jax.random.fold_in(key_of[1], 1), 0, 1)
    lags = jnp.clip(jax.random.uniform(key_of[2], (P_SIZE,), jnp.float32, -0.01, 0.01), -0.01, 0.01)
    drift = jnp.clip(jax.random.uniform(key_of[3], (P_SIZE,), jnp.float32, -4.0, 4.0), -4.0, 4.0)
    block_table = draw_block_table(jax.random.fold_in(key_of[5], 71), 0)
    return {"spectra": spectra, "valid": valid, "lags": lags, "drift": drift, "block_table": block_table}


full_turn = 2.0 * math.pi

def tile_partial(band_slab, band_id, pixel_lags, pixel_drift, time_coord, band_total, band_width):
    frequency = (band_id * band_width + jnp.arange(band_width, dtype=jnp.int32)).astype(jnp.float32)
    angle_grid = full_turn * frequency[:, None] * pixel_lags[None, :]
    cosine_grid = jnp.cos(angle_grid)
    sine_grid = jnp.sin(angle_grid)
    kernel = jnp.concatenate([jnp.concatenate([cosine_grid, -sine_grid], 1), jnp.concatenate([sine_grid, cosine_grid], 1)], 0).astype(jnp.bfloat16)
    product = jnp.dot(band_slab.astype(jnp.float32), kernel.astype(jnp.float32), precision=lax.Precision.HIGHEST, preferred_element_type=jnp.float32)
    columns = pixel_lags.shape[0]
    factor = full_turn * (band_id.astype(jnp.float32) + 0.5) / band_total
    rotation = (factor * pixel_drift)[None, :] * time_coord[:, None]
    return lax.optimization_barrier(jnp.sum(jnp.cos(rotation) * product[:, :columns] - jnp.sin(rotation) * product[:, columns:], axis=0))

def reference(spectra, valid, lags, drift, block_table):
    values = spectra.astype(jnp.float32)
    squares = lax.optimization_barrier(jnp.sum(values * values, axis=(2, 3, 4)))
    powers = squares.reshape(2, 2, SEGS).sum(axis=1) / F + 1e-06
    weight = valid.astype(jnp.float32) / (powers[0] * powers[1])
    hanford = jnp.concatenate([values[0], values[1]], axis=1)
    livingston = jnp.concatenate([values[2], values[3]], axis=1)
    cross_real = (hanford[:, :, 0] * livingston[:, :, 0] + hanford[:, :, 1] * livingston[:, :, 1]) * weight[:, None, None]
    cross_imag = (hanford[:, :, 0] * livingston[:, :, 1] - hanford[:, :, 1] * livingston[:, :, 0]) * weight[:, None, None]
    cross = jnp.stack([cross_real, cross_imag], 2).astype(jnp.bfloat16).reshape(SEGS, NBAND, 2 * BW)
    time_coord = (jnp.arange(SEGS, dtype=jnp.int32).astype(jnp.float32) + 0.5 - SEGS / 2) / SEGS

    def one_block(block_row):
        band_slab = lax.dynamic_index_in_dim(cross, block_row[0], 1, keepdims=False)
        pixel_start = block_row[1] * PT
        pixel_lags = lax.dynamic_slice_in_dim(lags, pixel_start, PT)
        pixel_drift = lax.dynamic_slice_in_dim(drift, pixel_start, PT)
        return tile_partial(band_slab, block_row[0], pixel_lags, pixel_drift, time_coord, NBAND, BW)
    partials = lax.map(one_block, block_table)
    summed = jax.ops.segment_sum(partials, block_table[:, 1], num_segments=NTILE)
    return summed.reshape(P_SIZE) / math.sqrt(SEGS * BW)
```

```python
import math

import jax
import jax.numpy as jnp
from jax import lax
from jax.experimental import pallas as pl
from jax.experimental.pallas import tpu as pltpu
from jax.sharding import PartitionSpec as P

MESH = pl.DeviceIdType.MESH

N_DET = 4
N_TM = 128
N_Z = 8
N_XY = 16
N_ZD = N_Z * N_DET
BINS = 128
BANDS = 32
TILES_OWN = 3
PIX_OWN = 96
CHUNKS = 8

SIN = [(-1.0) ** n * (2 * math.pi) ** (2 * n + 1) / math.factorial(2 * n + 1) for n in range(6)]
COS = [(-1.0) ** n * (2 * math.pi) ** (2 * n) / math.factorial(2 * n) for n in range(7)]


def horner(coefficients, x):
    total = jnp.full_like(x, coefficients[-1])
    for c in coefficients[-2::-1]:
        total = total * x + c
    return total


def cos_sin(turns):
    half = jnp.floor(turns * 2.0 + 0.5)
    r = turns - half * 0.5
    sign = 1.0 - 2.0 * (half - 2.0 * jnp.floor(half * 0.5))
    square = r * r
    return sign * horner(COS, square), sign * r * horner(SIN, square)


def iota(shape, dim):
    return lax.broadcasted_iota(jnp.int32, shape, dim)


def kernel(
    spec_hbm, valid_hbm, lags_hbm, drift_hbm, table_hbm, out_ref,
    own_v, other_v, lags_v, drift_v, table_v, table_s, valid_s,
    squares, squares_all, send1, recv1, send2, recv2,
    kmat, rot_cos, rot_sin, masks, part, parts, folded, send4, recv4,
    local_sem, hl_send, hl_recv, sq_send, sq_recv, s1_send, s1_recv,
    s2_send, s2_recv, s3_send, s3_recv, s4_send, s4_recv,
):
    det = lax.axis_index("det")
    tm = lax.axis_index("tm")
    k, h = det // 2, det % 2
    z, xy = tm // N_XY, tm % N_XY
    zd = z * N_DET + det

    def zd_peer(r):
        p = (zd + r) % N_ZD
        return (p % N_DET, p // N_DET * N_XY + xy)

    def xy_peer(r):
        return (det, z * N_XY + (xy + r) % N_XY)

    barrier = pltpu.get_barrier_semaphore()

    @pl.loop(1, N_ZD)
    def _(r):
        pl.semaphore_signal(barrier, inc=1, device_id=zd_peer(r), device_id_type=MESH)

    @pl.loop(1, N_XY)
    def _(r):
        pl.semaphore_signal(barrier, inc=1, device_id=xy_peer(r), device_id_type=MESH)

    loads = [
        pltpu.make_async_copy(src, dst, local_sem.at[n])
        for n, (src, dst) in enumerate(
            [
                (spec_hbm, own_v), (table_hbm, table_s), (table_hbm, table_v),
                (valid_hbm, valid_s), (lags_hbm, lags_v), (drift_hbm, drift_v),
            ]
        )
    ]
    for load in loads:
        load.start()
    loads[0].wait()

    own = own_v[...].astype(jnp.float32)
    sq = own * own
    row8 = iota((8, BINS), 0)
    seg0 = jnp.sum(sq[:64], axis=0, keepdims=True)
    seg1 = jnp.sum(sq[64:], axis=0, keepdims=True)
    sums = jnp.where(row8 == 0, seg0, jnp.where(row8 == 1, seg1, 0.0))
    squares[...] = sums
    squares_all[det] = sums

    pl.semaphore_wait(barrier, N_ZD - 1 + N_XY - 1)

    hl = pltpu.make_async_remote_copy(
        src_ref=own_v, dst_ref=other_v, send_sem=hl_send, recv_sem=hl_recv,
        device_id=((det + 2) % N_DET, tm), device_id_type=MESH,
    )
    hl.start()
    sq_copies = [
        pltpu.make_async_remote_copy(
            src_ref=squares, dst_ref=squares_all.at[det],
            send_sem=sq_send.at[r - 1], recv_sem=sq_recv.at[r - 1],
            device_id=((det + r) % N_DET, tm), device_id_type=MESH,
        )
        for r in range(1, N_DET)
    ]
    for copy in sq_copies:
        copy.start()
    for load in loads[1:]:
        load.wait()

    lane = iota((N_XY, BINS), 1)
    wanted = lane == 8 * iota((N_XY, BINS), 0) + 4 * h + 2 * k
    picks = []
    for dz in range(N_Z):
        bands = table_v[2 * dz : 2 * dz + 1, :].astype(jnp.float32)
        column = jnp.sum(jnp.where(wanted, bands, 0.0), axis=1, keepdims=True)
        picks.append((column - (BANDS * h).astype(jnp.float32)) * 2.0)
    pick = jnp.concatenate(picks, axis=0)
    source = iota((N_TM, BINS), 1).astype(jnp.float32)
    pick0 = jnp.where(source == pick, 1.0, 0.0).astype(jnp.bfloat16)
    pick1 = jnp.where(source == pick + 64.0, 1.0, 0.0).astype(jnp.bfloat16)

    hl.wait_recv()
    other = other_v[...].astype(jnp.float32)
    own_up = pltpu.roll(own, BINS - 1, 0)
    other_up = pltpu.roll(other, BINS - 1, 0)
    sign = (1 - 2 * k).astype(jnp.float32)
    cross_real = own * other + own_up * other_up
    cross_imag = (own * other_up - own_up * other) * sign
    for copy in sq_copies:
        copy.wait_recv()
    total = lambda a: jnp.sum(a, axis=1, keepdims=True) / 8192.0 + 1e-06
    power_h = total(squares_all[0] + squares_all[1])
    power_l = total(squares_all[2] + squares_all[3])
    flags = jnp.where(iota((8, 1), 0) == 0, valid_s[0], valid_s[1]).astype(jnp.float32)
    weight = flags / (power_h * power_l)
    weights = jnp.where(iota((BINS, 1), 0) < 64, weight[0:1], weight[1:2])
    cross = jnp.concatenate([cross_real * weights, cross_imag * weights], axis=1)
    cross = cross.astype(jnp.bfloat16)
    for s, p in enumerate((pick0, pick1)):
        rows = jnp.dot(p, cross, preferred_element_type=jnp.float32)
        rows = rows.astype(jnp.bfloat16).reshape(N_Z, N_XY, 2 * BINS)
        send1[:, :, 2 * BINS * s : 2 * BINS * (s + 1)] = rows

    def stage1(r):
        return pltpu.make_async_remote_copy(
            src_ref=send1.at[(z + r) % N_Z], dst_ref=recv1.at[z],
            send_sem=s1_send, recv_sem=s1_recv,
            device_id=(det, (z + r) % N_Z * N_XY + xy), device_id_type=MESH,
        )

    @pl.loop(1, N_Z)
    def _(r):
        stage1(r).start()

    recv1[z] = send1[z]

    g = table_s[2 * z, 8 * xy + 4 * h + 2 * k]
    g_f = g.astype(jnp.float32)
    first = [table_s[2 * z + 1, 8 * xy + 4 * h + 2 * k + n] for n in range(2)]
    col16 = iota((16, BINS), 0)
    col8 = iota((8, BINS), 0)

    @pl.loop(0, CHUNKS)
    def _(ch):
        tile = jnp.where(ch < 4, first[0], first[1])
        lag = lags_v[pl.ds(4 * tile + ch % 4, 1), :]
        ca, sa = cos_sin((g * BINS + 16 * col8).astype(jnp.float32) * lag)
        cb, sb = cos_sin(col16.astype(jnp.float32) * lag)
        for a in range(8):
            c1, s1 = ca[a : a + 1], sa[a : a + 1]
            cosine = (c1 * cb - s1 * sb).astype(jnp.bfloat16)
            sine = (s1 * cb + c1 * sb).astype(jnp.bfloat16)
            kmat[ch, 16 * a : 16 * a + 16, 0:BINS] = cosine
            kmat[ch, 16 * a : 16 * a + 16, BINS:] = -sine
            kmat[ch, BINS + 16 * a : BINS + 16 * a + 16, 0:BINS] = sine
            kmat[ch, BINS + 16 * a : BINS + 16 * a + 16, BINS:] = cosine

    pltpu.make_async_copy(
        recv1.at[pl.ds(0, N_Z - 1)], recv1.at[pl.ds(0, N_Z - 1)], s1_recv
    ).wait()

    o, n = iota((256, 256), 0), iota((256, 256), 1)
    perm = jnp.where(n == (o % 16 // 8) * 128 + (o % 8) * 16 + o // 16, 1.0, 0.0)
    perm = perm.astype(jnp.bfloat16)
    got = recv1[...].reshape(N_TM, 4 * BINS)
    got = jnp.concatenate([got[:, : 2 * BINS], got[:, 2 * BINS :]], axis=0)
    rows = jnp.dot(perm, got, preferred_element_type=jnp.float32).astype(jnp.bfloat16)
    send2[...] = rows.reshape(N_XY, 16, 2 * BINS)

    def stage2(r):
        return pltpu.make_async_remote_copy(
            src_ref=send2.at[(xy + r) % N_XY], dst_ref=recv2.at[xy],
            send_sem=s2_send, recv_sem=s2_recv,
            device_id=xy_peer(r), device_id_type=MESH,
        )

    @pl.loop(1, N_XY)
    def _(r):
        stage2(r).start()

    recv2[xy] = send2[xy]

    time_a = (32 * (col16 % 8) + col16 // 8).astype(jnp.float32) - 127.5
    time_b = (2 * col16).astype(jnp.float32)
    scale = (g_f + 0.5) * (1.0 / (64 * 256))

    @pl.loop(0, CHUNKS)
    def _(ch):
        tile = jnp.where(ch < 4, first[0], first[1])
        rate = drift_v[pl.ds(4 * tile + ch % 4, 1), :] * scale
        ca, sa = cos_sin(time_a * rate)
        cb, sb = cos_sin(time_b * rate)
        for a in range(16):
            c1, s1 = cb[a : a + 1], sb[a : a + 1]
            rot_cos[ch, 16 * a : 16 * a + 16, :] = c1 * ca - s1 * sa
            rot_sin[ch, 16 * a : 16 * a + 16, :] = s1 * ca + c1 * sa

    tile_mine = 24 * det + TILES_OWN * z

    @pl.loop(0, N_ZD)
    def _(p):
        at = 8 * xy + 4 * (p % 2) + p % 4 // 2 * 2
        t0 = table_s[2 * (p // 4) + 1, at]
        t1 = table_s[2 * (p // 4) + 1, at + 1]
        tiles = jnp.where(row8 < 4, t0, t1)
        for j in range(TILES_OWN):
            masks[p, j] = jnp.where(tiles == tile_mine + j, 1.0, 0.0)

    pltpu.make_async_copy(
        recv2.at[pl.ds(0, N_XY - 1)], recv2.at[pl.ds(0, N_XY - 1)], s2_recv
    ).wait()

    slab = recv2[...].reshape(256, 2 * BINS)

    for ch in range(CHUNKS):
        product = jnp.dot(slab, kmat[ch], preferred_element_type=jnp.float32)
        turned = rot_cos[ch] * product[:, :BINS] - rot_sin[ch] * product[:, BINS:]
        part[ch : ch + 1, :] = jnp.sum(turned, axis=0, keepdims=True)

    def stage3(r):
        return pltpu.make_async_remote_copy(
            src_ref=part, dst_ref=parts.at[zd],
            send_sem=s3_send, recv_sem=s3_recv,
            device_id=zd_peer(r), device_id_type=MESH,
        )

    @pl.loop(1, N_ZD)
    def _(r):
        stage3(r).start()

    parts[zd] = part[...]
    pltpu.make_async_copy(
        parts.at[pl.ds(0, N_ZD - 1)], parts.at[pl.ds(0, N_ZD - 1)], s3_recv
    ).wait()

    sums = [jnp.zeros((8, BINS), jnp.float32) for _ in range(TILES_OWN)]
    for p in range(N_ZD):
        terms = parts[p]
        for j in range(TILES_OWN):
            sums[j] += terms * masks[p, j]
    for j in range(TILES_OWN):
        folded[4 * j : 4 * j + 4, :] = sums[j][0:4] + sums[j][4:8]
    rows = [folded[pl.ds(i, 4, stride=3), :] for i in range(3)]
    lane4 = iota((4, BINS), 1)
    for y in range(4):
        at, shift = 96 * y // BINS, 96 * y % BINS
        low = pltpu.roll(rows[at], BINS - shift, 1) if shift else rows[at]
        if BINS - shift < PIX_OWN:
            high = pltpu.roll(rows[at + 1], BINS - shift, 1)
            low = jnp.where(lane4 < BINS - shift, low, high)
        for x in range(4):
            send4[4 * x + y] = low[x : x + 1]

    def stage4(r):
        return pltpu.make_async_remote_copy(
            src_ref=send4.at[(xy + r) % N_XY], dst_ref=recv4.at[xy],
            send_sem=s4_send, recv_sem=s4_recv,
            device_id=xy_peer(r), device_id_type=MESH,
        )

    @pl.loop(1, N_XY)
    def _(r):
        stage4(r).start()

    recv4[xy] = send4[xy]
    hl.wait_send()
    for copy in sq_copies:
        copy.wait_send()
    pltpu.make_async_copy(
        send1.at[pl.ds(0, N_Z - 1)], send1.at[pl.ds(0, N_Z - 1)], s1_send
    ).wait()
    pltpu.make_async_copy(
        send2.at[pl.ds(0, N_XY - 1)], send2.at[pl.ds(0, N_XY - 1)], s2_send
    ).wait()
    pltpu.make_async_copy(
        parts.at[pl.ds(0, N_ZD - 1)], parts.at[pl.ds(0, N_ZD - 1)], s3_send
    ).wait()
    pltpu.make_async_copy(
        send4.at[pl.ds(0, N_XY - 1)], send4.at[pl.ds(0, N_XY - 1)], s4_send
    ).wait()
    pltpu.make_async_copy(
        recv4.at[pl.ds(0, N_XY - 1)], recv4.at[pl.ds(0, N_XY - 1)], s4_recv
    ).wait()
    total = recv4[0]
    for q in range(1, N_XY):
        total += recv4[q]
    out_ref[...] = total * (1.0 / math.sqrt(256 * BINS))


def shards(spectra, valid, lags, drift, block_table):
    f32, bf16, i32 = jnp.float32, jnp.bfloat16, jnp.int32
    table = block_table.reshape(8, 128, 2).transpose(0, 2, 1).reshape(16, 128)
    dma = pltpu.SemaphoreType.DMA
    out = pl.pallas_call(
        kernel,
        out_shape=jax.ShapeDtypeStruct((1, BINS), f32),
        in_specs=[pl.BlockSpec(memory_space=pltpu.HBM)] * 5,
        out_specs=pl.BlockSpec(memory_space=pltpu.VMEM),
        scratch_shapes=[
            pltpu.VMEM((128, BINS), bf16),
            pltpu.VMEM((128, BINS), bf16),
            pltpu.VMEM((384, 128), f32),
            pltpu.VMEM((384, 128), f32),
            pltpu.VMEM((16, 128), i32),
            pltpu.SMEM((16, 128), i32),
            pltpu.SMEM((2,), i32),
            pltpu.VMEM((8, BINS), f32),
            pltpu.VMEM((N_DET, 8, BINS), f32),
            pltpu.VMEM((N_Z, N_XY, 4 * BINS), bf16),
            pltpu.VMEM((N_Z, N_XY, 4 * BINS), bf16),
            pltpu.VMEM((N_XY, 16, 2 * BINS), bf16),
            pltpu.VMEM((N_XY, 16, 2 * BINS), bf16),
            pltpu.VMEM((CHUNKS, 256, 256), bf16),
            pltpu.VMEM((CHUNKS, 256, BINS), f32),
            pltpu.VMEM((CHUNKS, 256, BINS), f32),
            pltpu.VMEM((N_ZD, TILES_OWN, 8, BINS), f32),
            pltpu.VMEM((8, BINS), f32),
            pltpu.VMEM((N_ZD, 8, BINS), f32),
            pltpu.VMEM((16, BINS), f32),
            pltpu.VMEM((N_XY, 1, BINS), f32),
            pltpu.VMEM((N_XY, 1, BINS), f32),
            dma((6,)), dma, dma, dma((3,)), dma((3,)), dma, dma,
            dma, dma, dma, dma, dma, dma,
        ],
        compiler_params=pltpu.CompilerParams(
            collective_id=0, has_side_effects=True, vmem_limit_bytes=32 * 1024 * 1024
        ),
        name="radiometer",
    )(
        spectra.reshape(128, BINS),
        valid,
        lags.reshape(384, 128),
        drift.reshape(384, 128),
        table,
    )
    return out.reshape(BINS)[:PIX_OWN]


def solution(mesh):
    placed = (P("det", "tm", None, None, None), P("tm"), P(), P(), P())
    return jax.shard_map(
        shards, mesh=mesh, in_specs=placed, out_specs=P(("det", "tm")), check_vma=False
    )
```

```python
import math

import jax
import jax.numpy as jnp
from jax import lax
from jax.experimental import pallas as pl
from jax.experimental.pallas import tpu as pltpu
from jax.sharding import PartitionSpec as P

MESH = pl.DeviceIdType.MESH

N_DET = 4
N_TM = 128
N_Z = 8
N_XY = 16
N_ZH = 16
N_XYK = 32
BINS = 128
BANDS = 32
TILES_OWN = 3
TILES_SUM = 6
PIX_OWN = 96
CHUNKS = 8

SIN = [(-1.0) ** n * (2 * math.pi) ** (2 * n + 1) / math.factorial(2 * n + 1) for n in range(6)]
COS = [(-1.0) ** n * (2 * math.pi) ** (2 * n) / math.factorial(2 * n) for n in range(7)]


def horner(coefficients, x):
    total = jnp.full_like(x, coefficients[-1])
    for c in coefficients[-2::-1]:
        total = total * x + c
    return total


def cos_sin(turns):
    half = jnp.floor(turns * 2.0 + 0.5)
    r = turns - half * 0.5
    sign = 1.0 - 2.0 * (half - 2.0 * jnp.floor(half * 0.5))
    square = r * r
    return sign * horner(COS, square), sign * r * horner(SIN, square)


def iota(shape, dim):
    return lax.broadcasted_iota(jnp.int32, shape, dim)


def kernel(
    spec_hbm, valid_hbm, lags_hbm, drift_hbm, table_hbm, out_ref,
    own_v, other_v, lags_v, drift_v, table_v, table_s, valid_s,
    squares, squares_all, send2, recv2,
    kmat, rot_cos, rot_sin, masks, part, parts, folded, send4, recv4,
    local_sem, hl_send, hl_recv, sq_send, sq_recv,
    s2_send, s2_recv, s3_send, s3_recv, s4_send, s4_recv, plane_sem, space_sem,
):
    det = lax.axis_index("det")
    tm = lax.axis_index("tm")
    k, h = det // 2, det % 2
    z, xy = tm // N_XY, tm % N_XY
    x, y = xy // 4, xy % 4
    yk = y * 2 + k
    zh = z * 2 + h
    xyk = xy * 2 + k

    def z_peer(r):
        return (det, (z + r) % N_Z * N_XY + xy)

    def x_peer(r):
        return (det, z * N_XY + (x + r) % 4 * 4 + y)

    def y_peer(r):
        p = (yk + r) % 8
        return (p % 2 * 2 + h, z * N_XY + x * 4 + p // 2)

    def zh_peer(r):
        p = (zh + r) % N_ZH
        return (k * 2 + p % 2, p // 2 * N_XY + xy)

    def xyk_peer(r):
        p = (xyk + r) % N_XYK
        return (p % 2 * 2 + h, z * N_XY + p // 2)

    core_peer = (k * 2 + 1 - h, tm)
    across_peer = (3 - det, tm)

    barrier = pltpu.get_barrier_semaphore()

    def tell(semaphore, peer):
        pl.semaphore_signal(semaphore, inc=1, device_id=peer, device_id_type=MESH)

    @pl.loop(1, N_Z)
    def _(r):
        tell(barrier, z_peer(r))

    @pl.loop(1, 8)
    def _(r):
        tell(barrier, y_peer(r))

    @pl.loop(1, 4)
    def _(r):
        tell(barrier, x_peer(r))

    tell(barrier, core_peer)
    tell(barrier, across_peer)

    loads = [
        pltpu.make_async_copy(src, dst, local_sem.at[n])
        for n, (src, dst) in enumerate(
            [
                (spec_hbm, own_v), (table_hbm, table_s), (table_hbm, table_v),
                (valid_hbm, valid_s), (lags_hbm, lags_v), (drift_hbm, drift_v),
            ]
        )
    ]
    for load in loads:
        load.start()
    loads[0].wait()

    own = own_v[...].astype(jnp.float32)
    sq = own * own
    row8 = iota((8, BINS), 0)
    seg0 = jnp.sum(sq[:64], axis=0, keepdims=True)
    seg1 = jnp.sum(sq[64:], axis=0, keepdims=True)
    sums = jnp.where(row8 == 0, seg0, jnp.where(row8 == 1, seg1, 0.0))
    squares[...] = sums
    squares_all[det] = sums

    pl.semaphore_wait(barrier, 7 + 7 + 3 + 2)

    hl = pltpu.make_async_remote_copy(
        src_ref=own_v, dst_ref=other_v, send_sem=hl_send, recv_sem=hl_recv,
        device_id=((det + 2) % N_DET, tm), device_id_type=MESH,
    )
    hl.start()
    sq_copies = [
        pltpu.make_async_remote_copy(
            src_ref=squares, dst_ref=squares_all.at[det],
            send_sem=sq_send.at[r - 1], recv_sem=sq_recv.at[r - 1],
            device_id=((det + r) % N_DET, tm), device_id_type=MESH,
        )
        for r in range(1, N_DET)
    ]
    for copy in sq_copies:
        copy.start()

    @pl.loop(1, 4)
    def _(r):
        tell(plane_sem, x_peer(r))

    tell(plane_sem, core_peer)
    for load in loads[1:]:
        load.wait()

    bands = table_v[...].astype(jnp.float32)
    target = iota((4 * N_TM, BINS), 0)
    wanted = iota((4 * N_XY, BINS), 1) == (
        8 * (iota((4 * N_XY, BINS), 0) // 4) + 4 * h + 2 * k
    )
    picks = []
    for dz in range(N_Z):
        column = jnp.where(wanted, bands[2 * dz : 2 * dz + 1], 0.0)
        picks.append(jnp.sum(column, axis=1, keepdims=True))
    pick = (jnp.concatenate(picks, axis=0) - (BANDS * h).astype(jnp.float32)) * 2.0
    segment = (target[:, 0:1] // 2 % 2).astype(jnp.float32) * 64.0
    is_imag = target[:, 0:1] % 2
    source = iota((4 * N_TM, BINS), 1).astype(jnp.float32)
    chosen = jnp.where(source == pick + segment, 1.0, 0.0)
    pick_real = jnp.where(is_imag == 0, chosen, 0.0).astype(jnp.bfloat16)
    pick_imag = jnp.where(is_imag == 1, chosen, 0.0).astype(jnp.bfloat16)
    pick = jnp.concatenate([pick_real, pick_imag], axis=1)

    pl.semaphore_wait(plane_sem, 4)

    @pl.loop(1, N_Z)
    def _(r):
        tell(space_sem, z_peer(r))

    hl.wait_recv()
    other = other_v[...].astype(jnp.float32)
    own_up = pltpu.roll(own, BINS - 1, 0)
    other_up = pltpu.roll(other, BINS - 1, 0)
    sign = (1 - 2 * k).astype(jnp.float32)
    cross_real = own * other + own_up * other_up
    cross_imag = (own * other_up - own_up * other) * sign
    for copy in sq_copies:
        copy.wait_recv()
    total = lambda a: jnp.sum(a, axis=1, keepdims=True) / 8192.0 + 1e-06
    power_h = total(squares_all[0] + squares_all[1])
    power_l = total(squares_all[2] + squares_all[3])
    flags = jnp.where(iota((8, 1), 0) == 0, valid_s[0], valid_s[1]).astype(jnp.float32)
    weight = flags / (power_h * power_l)
    weights = jnp.where(iota((BINS, 1), 0) < 64, weight[0:1], weight[1:2])
    cross = jnp.concatenate([cross_real * weights, cross_imag * weights], axis=0)
    rows = jnp.dot(pick, cross.astype(jnp.bfloat16), preferred_element_type=jnp.float32)
    send2.reshape(4 * N_TM, BINS)[...] = rows.astype(jnp.bfloat16)

    pl.semaphore_wait(space_sem, N_Z - 1)

    def stage2(r):
        to = (tm + r) % N_TM
        return pltpu.make_async_remote_copy(
            src_ref=send2.at[to], dst_ref=recv2.at[tm],
            send_sem=s2_send, recv_sem=s2_recv,
            device_id=(det, to), device_id_type=MESH,
        )

    @pl.loop(1, N_TM)
    def _(r):
        stage2(r).start()

    recv2[tm] = send2[tm]

    g = table_s[2 * z, 8 * xy + 4 * h + 2 * k]
    g_f = g.astype(jnp.float32)
    first = [table_s[2 * z + 1, 8 * xy + 4 * h + 2 * k + n] for n in range(2)]
    col16 = iota((16, BINS), 0)
    col8 = iota((8, BINS), 0)

    @pl.loop(0, CHUNKS)
    def _(ch):
        tile = jnp.where(ch < 4, first[0], first[1])
        lag = lags_v[pl.ds(4 * tile + ch % 4, 1), :]
        ca, sa = cos_sin((g * BINS + 16 * col8).astype(jnp.float32) * lag)
        cb, sb = cos_sin(col16.astype(jnp.float32) * lag)
        for a in range(8):
            c1, s1 = ca[a : a + 1], sa[a : a + 1]
            cosine = (c1 * cb - s1 * sb).astype(jnp.bfloat16)
            sine = (s1 * cb + c1 * sb).astype(jnp.bfloat16)
            kmat[ch, 16 * a : 16 * a + 16, 0:BINS] = cosine
            kmat[ch, 16 * a : 16 * a + 16, BINS:] = -sine
            kmat[ch, BINS + 16 * a : BINS + 16 * a + 16, 0:BINS] = sine
            kmat[ch, BINS + 16 * a : BINS + 16 * a + 16, BINS:] = cosine

    time_a = (16 * col16).astype(jnp.float32) - 127.5
    time_b = (2 * (col16 % 8) + col16 // 8).astype(jnp.float32)
    scale = (g_f + 0.5) * (1.0 / (64 * 256))

    @pl.loop(0, CHUNKS)
    def _(ch):
        tile = jnp.where(ch < 4, first[0], first[1])
        rate = drift_v[pl.ds(4 * tile + ch % 4, 1), :] * scale
        ca, sa = cos_sin(time_a * rate)
        cb, sb = cos_sin(time_b * rate)
        for a in range(16):
            c1, s1 = ca[a : a + 1], sa[a : a + 1]
            cosine = c1 * cb - s1 * sb
            sine = s1 * cb + c1 * sb
            for s in range(2):
                at = s * N_TM + 8 * a
                rot_cos[ch, at : at + 8, :] = cosine[8 * s : 8 * s + 8]
                rot_sin[ch, at : at + 8, :] = sine[8 * s : 8 * s + 8]

    @pl.loop(0, N_ZH)
    def _(p):
        at = 8 * xy + 4 * (p % 2) + 2 * k
        t0 = table_s[2 * (p // 2) + 1, at]
        t1 = table_s[2 * (p // 2) + 1, at + 1]
        tiles = jnp.where(row8 < 4, t0, t1)
        for j in range(TILES_SUM):
            tile = 24 * (j // 3 * 2 + h) + 3 * z + j % 3
            masks[p, j] = jnp.where(tiles == tile, 1.0, 0.0)

    o, n = iota((256, 512), 0), iota((256, 512), 1)
    want = 4 * (o % N_TM) + 2 * (o // N_TM)
    perms = [
        jnp.where(n == want + c, 1.0, 0.0).astype(jnp.bfloat16) for c in range(2)
    ]

    pltpu.make_async_copy(
        recv2.at[pl.ds(0, N_TM - 1)], recv2.at[pl.ds(0, N_TM - 1)], s2_recv
    ).wait()

    got = recv2.reshape(4 * N_TM, BINS)[...]
    slab = jnp.concatenate(
        [jnp.dot(p, got, preferred_element_type=jnp.float32) for p in perms], axis=1
    ).astype(jnp.bfloat16)

    for ch in range(CHUNKS):
        product = jnp.dot(slab, kmat[ch], preferred_element_type=jnp.float32)
        turned = rot_cos[ch] * product[:, :BINS] - rot_sin[ch] * product[:, BINS:]
        part[ch : ch + 1, :] = jnp.sum(turned, axis=0, keepdims=True)

    def stage3(r):
        return pltpu.make_async_remote_copy(
            src_ref=part, dst_ref=parts.at[zh],
            send_sem=s3_send, recv_sem=s3_recv,
            device_id=zh_peer(r), device_id_type=MESH,
        )

    @pl.loop(1, N_ZH)
    def _(r):
        stage3(r).start()

    parts[zh] = part[...]
    pltpu.make_async_copy(
        parts.at[pl.ds(0, N_ZH - 1)], parts.at[pl.ds(0, N_ZH - 1)], s3_recv
    ).wait()

    sums = [jnp.zeros((8, BINS), jnp.float32) for _ in range(TILES_SUM)]
    for p in range(N_ZH):
        terms = parts[p]
        for j in range(TILES_SUM):
            sums[j] += terms * masks[p, j]
    for j in range(TILES_SUM):
        at = 16 * (j // 3) + 4 * (j % 3)
        folded[at : at + 4, :] = sums[j][0:4] + sums[j][4:8]
    lane4 = iota((4, BINS), 1)
    for q in range(2):
        rows = [folded[pl.ds(16 * q + i, 4, stride=3), :] for i in range(3)]
        for j in range(4):
            at, shift = 96 * j // BINS, 96 * j % BINS
            low = pltpu.roll(rows[at], BINS - shift, 1) if shift else rows[at]
            if BINS - shift < PIX_OWN:
                high = pltpu.roll(rows[at + 1], BINS - shift, 1)
                low = jnp.where(lane4 < BINS - shift, low, high)
            for i in range(4):
                send4[(4 * i + j) * 2 + q] = low[i : i + 1]

    def stage4(r):
        return pltpu.make_async_remote_copy(
            src_ref=send4.at[(xyk + r) % N_XYK], dst_ref=recv4.at[xyk],
            send_sem=s4_send, recv_sem=s4_recv,
            device_id=xyk_peer(r), device_id_type=MESH,
        )

    @pl.loop(1, N_XYK)
    def _(r):
        stage4(r).start()

    recv4[xyk] = send4[xyk]
    hl.wait_send()
    for copy in sq_copies:
        copy.wait_send()
    pltpu.make_async_copy(
        send2.at[pl.ds(0, N_TM - 1)], send2.at[pl.ds(0, N_TM - 1)], s2_send
    ).wait()
    pltpu.make_async_copy(
        parts.at[pl.ds(0, N_ZH - 1)], parts.at[pl.ds(0, N_ZH - 1)], s3_send
    ).wait()
    pltpu.make_async_copy(
        send4.at[pl.ds(0, N_XYK - 1)], send4.at[pl.ds(0, N_XYK - 1)], s4_send
    ).wait()
    pltpu.make_async_copy(
        recv4.at[pl.ds(0, N_XYK - 1)], recv4.at[pl.ds(0, N_XYK - 1)], s4_recv
    ).wait()
    total = recv4[0]
    for q in range(1, N_XYK):
        total += recv4[q]
    out_ref[...] = total * (1.0 / math.sqrt(256 * BINS))


def shards(spectra, valid, lags, drift, block_table):
    f32, bf16, i32 = jnp.float32, jnp.bfloat16, jnp.int32
    table = block_table.reshape(8, 128, 2).transpose(0, 2, 1).reshape(16, 128)
    dma = pltpu.SemaphoreType.DMA
    out = pl.pallas_call(
        kernel,
        out_shape=jax.ShapeDtypeStruct((1, BINS), f32),
        in_specs=[pl.BlockSpec(memory_space=pltpu.HBM)] * 5,
        out_specs=pl.BlockSpec(memory_space=pltpu.VMEM),
        scratch_shapes=[
            pltpu.VMEM((128, BINS), bf16),
            pltpu.VMEM((128, BINS), bf16),
            pltpu.VMEM((384, 128), f32),
            pltpu.VMEM((384, 128), f32),
            pltpu.VMEM((16, 128), i32),
            pltpu.SMEM((16, 128), i32),
            pltpu.SMEM((2,), i32),
            pltpu.VMEM((8, BINS), f32),
            pltpu.VMEM((N_DET, 8, BINS), f32),
            pltpu.VMEM((N_TM, 4, BINS), bf16),
            pltpu.VMEM((N_TM, 4, BINS), bf16),
            pltpu.VMEM((CHUNKS, 256, 256), bf16),
            pltpu.VMEM((CHUNKS, 256, BINS), f32),
            pltpu.VMEM((CHUNKS, 256, BINS), f32),
            pltpu.VMEM((N_ZH, TILES_SUM, 8, BINS), f32),
            pltpu.VMEM((8, BINS), f32),
            pltpu.VMEM((N_ZH, 8, BINS), f32),
            pltpu.VMEM((32, BINS), f32),
            pltpu.VMEM((N_XYK, 1, BINS), f32),
            pltpu.VMEM((N_XYK, 1, BINS), f32),
            dma((6,)), dma, dma, dma((3,)), dma((3,)), dma, dma, dma, dma, dma, dma,
            pltpu.SemaphoreType.REGULAR, pltpu.SemaphoreType.REGULAR,
        ],
        compiler_params=pltpu.CompilerParams(
            collective_id=0, has_side_effects=True, vmem_limit_bytes=60 * 1024 * 1024
        ),
        name="radiometer",
    )(
        spectra.reshape(128, BINS),
        valid,
        lags.reshape(384, 128),
        drift.reshape(384, 128),
        table,
    )
    return out.reshape(BINS)[:PIX_OWN]


def solution(mesh):
    placed = (P("det", "tm", None, None, None), P("tm"), P(), P(), P())
    return jax.shard_map(
        shards, mesh=mesh, in_specs=placed, out_specs=P(("det", "tm")), check_vma=False
    )
```

```python
import math

import jax
import jax.numpy as jnp
from jax import lax
from jax.experimental import pallas as pl
from jax.experimental.pallas import tpu as pltpu
from jax.sharding import PartitionSpec as P

MESH = pl.DeviceIdType.MESH

N_DET = 4
N_TM = 128
N_Z = 8
N_XY = 16
N_ZH = 16
N_XYK = 32
BINS = 128
BANDS = 32
TILES_OWN = 3
TILES_SUM = 6
PIX_OWN = 96
CHUNKS = 8

SIN = [(-1.0) ** n * (2 * math.pi) ** (2 * n + 1) / math.factorial(2 * n + 1) for n in range(6)]
COS = [(-1.0) ** n * (2 * math.pi) ** (2 * n) / math.factorial(2 * n) for n in range(7)]


def horner(coefficients, x):
    total = jnp.full_like(x, coefficients[-1])
    for c in coefficients[-2::-1]:
        total = total * x + c
    return total


def cos_sin(turns):
    half = jnp.floor(turns * 2.0 + 0.5)
    r = turns - half * 0.5
    sign = 1.0 - 2.0 * (half - 2.0 * jnp.floor(half * 0.5))
    square = r * r
    return sign * horner(COS, square), sign * r * horner(SIN, square)


def iota(shape, dim):
    return lax.broadcasted_iota(jnp.int32, shape, dim)


def kernel(
    spec_hbm, valid_hbm, lags_hbm, drift_hbm, table_hbm, out_ref,
    own_v, other_v, lags_v, drift_v, table_v, table_s, valid_s,
    squares, squares_all, send2, recv2,
    kmat, rot_cos, rot_sin, masks, part, parts, folded, send4, recv4,
    local_sem, hl_send, hl_recv, sq_send, sq_recv,
    s2_send, s2_recv, s3_send, s3_recv, s4_send, s4_recv, plane_sem, space_sem,
):
    det = lax.axis_index("det")
    tm = lax.axis_index("tm")
    k, h = det // 2, det % 2
    z, xy = tm // N_XY, tm % N_XY
    x, y = xy // 4, xy % 4
    yk = y * 2 + k
    zh = z * 2 + h
    xyk = xy * 2 + k

    def z_peer(r):
        return (det, (z + r) % N_Z * N_XY + xy)

    def x_peer(r):
        return (det, z * N_XY + (x + r) % 4 * 4 + y)

    def y_peer(r):
        p = (yk + r) % 8
        return (p % 2 * 2 + h, z * N_XY + x * 4 + p // 2)

    def zh_peer(r):
        p = (zh + r) % N_ZH
        return (k * 2 + p % 2, p // 2 * N_XY + xy)

    def xyk_peer(r):
        p = (xyk + r) % N_XYK
        return (p % 2 * 2 + h, z * N_XY + p // 2)

    step = 2 * k - 1

    def chip_at(distance):
        chip = (yk + step * distance + 8) % 8
        return chip % 2 * 2 + h, chip // 2

    sent_to = [chip_at(j) for j in range(4)]
    core_peer = (k * 2 + 1 - h, tm)
    across_peer = (3 - det, tm)

    barrier = pltpu.get_barrier_semaphore()

    def tell(semaphore, peer):
        pl.semaphore_signal(semaphore, inc=1, device_id=peer, device_id_type=MESH)

    @pl.loop(1, N_Z)
    def _(r):
        tell(barrier, z_peer(r))

    @pl.loop(1, 8)
    def _(r):
        tell(barrier, y_peer(r))

    @pl.loop(1, 4)
    def _(r):
        tell(barrier, x_peer(r))

    tell(barrier, core_peer)
    tell(barrier, across_peer)

    loads = [
        pltpu.make_async_copy(src, dst, local_sem.at[n])
        for n, (src, dst) in enumerate(
            [
                (spec_hbm, own_v), (table_hbm, table_s), (table_hbm, table_v),
                (valid_hbm, valid_s), (lags_hbm, lags_v), (drift_hbm, drift_v),
            ]
        )
    ]
    for load in loads:
        load.start()
    loads[0].wait()

    own = own_v[...].astype(jnp.float32)
    sq = own * own
    row8 = iota((8, BINS), 0)
    seg0 = jnp.sum(sq[:64], axis=0, keepdims=True)
    seg1 = jnp.sum(sq[64:], axis=0, keepdims=True)
    sums = jnp.where(row8 == 0, seg0, jnp.where(row8 == 1, seg1, 0.0))
    squares[...] = sums
    squares_all[det] = sums

    for load in loads[1:]:
        load.wait()

    bands = table_v[...].astype(jnp.float32)
    target = iota((4 * N_TM, BINS), 0)
    row = iota((4 * N_XY, BINS), 0)
    chip = (yk + step * (row // 4 % 4) + 8) % 8
    at = 32 * (row // 16) + 8 * (chip // 2) + 2 * (chip % 2) + 4 * h
    wanted = iota((4 * N_XY, BINS), 1) == at
    picks = []
    for dz in range(N_Z):
        column = jnp.where(wanted, bands[2 * dz : 2 * dz + 1], 0.0)
        picks.append(jnp.sum(column, axis=1, keepdims=True))
    pick = (jnp.concatenate(picks, axis=0) - (BANDS * h).astype(jnp.float32)) * 2.0
    segment = (target[:, 0:1] // 2 % 2).astype(jnp.float32) * 64.0
    is_imag = target[:, 0:1] % 2
    source = iota((4 * N_TM, BINS), 1).astype(jnp.float32)
    chosen = jnp.where(source == pick + segment, 1.0, 0.0)
    pick_real = jnp.where(is_imag == 0, chosen, 0.0).astype(jnp.bfloat16)
    pick_imag = jnp.where(is_imag == 1, chosen, 0.0).astype(jnp.bfloat16)
    pick = jnp.concatenate([pick_real, pick_imag], axis=1)

    pl.semaphore_wait(barrier, 7 + 7 + 3 + 2)

    @pl.loop(1, 4)
    def _(r):
        tell(plane_sem, x_peer(r))

    tell(plane_sem, core_peer)

    hl = pltpu.make_async_remote_copy(
        src_ref=own_v, dst_ref=other_v, send_sem=hl_send, recv_sem=hl_recv,
        device_id=((det + 2) % N_DET, tm), device_id_type=MESH,
    )
    hl.start()
    sq_copies = [
        pltpu.make_async_remote_copy(
            src_ref=squares, dst_ref=squares_all.at[det],
            send_sem=sq_send.at[r - 1], recv_sem=sq_recv.at[r - 1],
            device_id=((det + r) % N_DET, tm), device_id_type=MESH,
        )
        for r in range(1, N_DET)
    ]
    for copy in sq_copies:
        copy.start()

    pl.semaphore_wait(plane_sem, 4)

    for distance in (1, 3, -2):
        d, chip_y = chip_at(distance)
        tell(space_sem, (d, z * N_XY + x * 4 + chip_y))

    hl.wait_recv()
    other = other_v[...].astype(jnp.float32)
    own_up = pltpu.roll(own, BINS - 1, 0)
    other_up = pltpu.roll(other, BINS - 1, 0)
    sign = (1 - 2 * k).astype(jnp.float32)
    cross_real = own * other + own_up * other_up
    cross_imag = (own * other_up - own_up * other) * sign
    for copy in sq_copies:
        copy.wait_recv()
    total = lambda a: jnp.sum(a, axis=1, keepdims=True) / 8192.0 + 1e-06
    power_h = total(squares_all[0] + squares_all[1])
    power_l = total(squares_all[2] + squares_all[3])
    flags = jnp.where(iota((8, 1), 0) == 0, valid_s[0], valid_s[1]).astype(jnp.float32)
    weight = flags / (power_h * power_l)
    weights = jnp.where(iota((BINS, 1), 0) < 64, weight[0:1], weight[1:2])
    cross = jnp.concatenate([cross_real * weights, cross_imag * weights], axis=0)
    rows = jnp.dot(pick, cross.astype(jnp.bfloat16), preferred_element_type=jnp.float32)
    send2.reshape(4 * N_TM, BINS)[...] = rows.astype(jnp.bfloat16)

    zx = z * 4 + x

    def stage2(to_zx, j):
        d, chip_y = sent_to[j]
        return pltpu.make_async_remote_copy(
            src_ref=send2.at[4 * to_zx + j], dst_ref=recv2.at[tm],
            send_sem=s2_send, recv_sem=s2_recv,
            device_id=(d, 4 * to_zx + chip_y), device_id_type=MESH,
        )

    pl.semaphore_wait(space_sem, 3)

    for j in range(1, 4):
        stage2(zx, j).start()

    @pl.loop(1, 32)
    def _(r):
        for j in range(4):
            stage2((zx + r) % 32, j).start()

    recv2[tm] = send2[4 * zx]

    g = table_s[2 * z, 8 * xy + 4 * h + 2 * k]
    g_f = g.astype(jnp.float32)
    first = [table_s[2 * z + 1, 8 * xy + 4 * h + 2 * k + n] for n in range(2)]
    col16 = iota((16, BINS), 0)
    col8 = iota((8, BINS), 0)

    @pl.loop(0, CHUNKS)
    def _(ch):
        tile = jnp.where(ch < 4, first[0], first[1])
        lag = lags_v[pl.ds(4 * tile + ch % 4, 1), :]
        ca, sa = cos_sin((g * BINS + 16 * col8).astype(jnp.float32) * lag)
        cb, sb = cos_sin(col16.astype(jnp.float32) * lag)
        for a in range(8):
            c1, s1 = ca[a : a + 1], sa[a : a + 1]
            cosine = (c1 * cb - s1 * sb).astype(jnp.bfloat16)
            sine = (s1 * cb + c1 * sb).astype(jnp.bfloat16)
            kmat[ch, 16 * a : 16 * a + 16, 0:BINS] = cosine
            kmat[ch, 16 * a : 16 * a + 16, BINS:] = -sine
            kmat[ch, BINS + 16 * a : BINS + 16 * a + 16, 0:BINS] = sine
            kmat[ch, BINS + 16 * a : BINS + 16 * a + 16, BINS:] = cosine

    time_a = (16 * col16).astype(jnp.float32) - 127.5
    time_b = (2 * (col16 % 8) + col16 // 8).astype(jnp.float32)
    scale = (g_f + 0.5) * (1.0 / (64 * 256))

    @pl.loop(0, CHUNKS)
    def _(ch):
        tile = jnp.where(ch < 4, first[0], first[1])
        rate = drift_v[pl.ds(4 * tile + ch % 4, 1), :] * scale
        ca, sa = cos_sin(time_a * rate)
        cb, sb = cos_sin(time_b * rate)
        for a in range(16):
            c1, s1 = ca[a : a + 1], sa[a : a + 1]
            cosine = c1 * cb - s1 * sb
            sine = s1 * cb + c1 * sb
            for s in range(2):
                at = s * N_TM + 8 * a
                rot_cos[ch, at : at + 8, :] = cosine[8 * s : 8 * s + 8]
                rot_sin[ch, at : at + 8, :] = sine[8 * s : 8 * s + 8]

    @pl.loop(0, N_ZH)
    def _(p):
        at = 8 * xy + 4 * (p % 2) + 2 * k
        t0 = table_s[2 * (p // 2) + 1, at]
        t1 = table_s[2 * (p // 2) + 1, at + 1]
        tiles = jnp.where(row8 < 4, t0, t1)
        for j in range(TILES_SUM):
            tile = 24 * (j // 3 * 2 + h) + 3 * z + j % 3
            masks[p, j] = jnp.where(tiles == tile, 1.0, 0.0)

    o, n = iota((256, 512), 0), iota((256, 512), 1)
    want = 4 * (o % N_TM) + 2 * (o // N_TM)
    perms = [
        jnp.where(n == want + c, 1.0, 0.0).astype(jnp.bfloat16) for c in range(2)
    ]

    pltpu.make_async_copy(
        recv2.at[pl.ds(0, N_TM - 1)], recv2.at[pl.ds(0, N_TM - 1)], s2_recv
    ).wait()

    got = recv2.reshape(4 * N_TM, BINS)[...]
    slab = jnp.concatenate(
        [jnp.dot(p, got, preferred_element_type=jnp.float32) for p in perms], axis=1
    ).astype(jnp.bfloat16)

    for ch in range(CHUNKS):
        product = jnp.dot(slab, kmat[ch], preferred_element_type=jnp.float32)
        turned = rot_cos[ch] * product[:, :BINS] - rot_sin[ch] * product[:, BINS:]
        part[ch : ch + 1, :] = jnp.sum(turned, axis=0, keepdims=True)

    def stage3(r):
        return pltpu.make_async_remote_copy(
            src_ref=part, dst_ref=parts.at[zh],
            send_sem=s3_send, recv_sem=s3_recv,
            device_id=zh_peer(r), device_id_type=MESH,
        )

    @pl.loop(1, N_ZH)
    def _(r):
        stage3(r).start()

    parts[zh] = part[...]
    pltpu.make_async_copy(
        parts.at[pl.ds(0, N_ZH - 1)], parts.at[pl.ds(0, N_ZH - 1)], s3_recv
    ).wait()

    sums = [jnp.zeros((8, BINS), jnp.float32) for _ in range(TILES_SUM)]
    for p in range(N_ZH):
        terms = parts[p]
        for j in range(TILES_SUM):
            sums[j] += terms * masks[p, j]
    for j in range(TILES_SUM):
        at = 16 * (j // 3) + 4 * (j % 3)
        folded[at : at + 4, :] = sums[j][0:4] + sums[j][4:8]
    lane4 = iota((4, BINS), 1)
    for q in range(2):
        rows = [folded[pl.ds(16 * q + i, 4, stride=3), :] for i in range(3)]
        for j in range(4):
            at, shift = 96 * j // BINS, 96 * j % BINS
            low = pltpu.roll(rows[at], BINS - shift, 1) if shift else rows[at]
            if BINS - shift < PIX_OWN:
                high = pltpu.roll(rows[at + 1], BINS - shift, 1)
                low = jnp.where(lane4 < BINS - shift, low, high)
            for i in range(4):
                send4[(4 * i + j) * 2 + q] = low[i : i + 1]

    def stage4(r):
        return pltpu.make_async_remote_copy(
            src_ref=send4.at[(xyk + r) % N_XYK], dst_ref=recv4.at[xyk],
            send_sem=s4_send, recv_sem=s4_recv,
            device_id=xyk_peer(r), device_id_type=MESH,
        )

    @pl.loop(1, N_XYK)
    def _(r):
        stage4(r).start()

    recv4[xyk] = send4[xyk]
    hl.wait_send()
    for copy in sq_copies:
        copy.wait_send()
    pltpu.make_async_copy(
        send2.at[pl.ds(0, N_TM - 1)], send2.at[pl.ds(0, N_TM - 1)], s2_send
    ).wait()
    pltpu.make_async_copy(
        parts.at[pl.ds(0, N_ZH - 1)], parts.at[pl.ds(0, N_ZH - 1)], s3_send
    ).wait()
    pltpu.make_async_copy(
        send4.at[pl.ds(0, N_XYK - 1)], send4.at[pl.ds(0, N_XYK - 1)], s4_send
    ).wait()
    pltpu.make_async_copy(
        recv4.at[pl.ds(0, N_XYK - 1)], recv4.at[pl.ds(0, N_XYK - 1)], s4_recv
    ).wait()
    total = recv4[0]
    for q in range(1, N_XYK):
        total += recv4[q]
    out_ref[...] = total * (1.0 / math.sqrt(256 * BINS))


def shards(spectra, valid, lags, drift, block_table):
    f32, bf16, i32 = jnp.float32, jnp.bfloat16, jnp.int32
    table = block_table.reshape(8, 128, 2).transpose(0, 2, 1).reshape(16, 128)
    dma = pltpu.SemaphoreType.DMA
    out = pl.pallas_call(
        kernel,
        out_shape=pltpu.VMEM((1, BINS), f32),
        in_specs=[pl.BlockSpec(memory_space=pltpu.HBM)] * 5,
        out_specs=pl.BlockSpec(memory_space=pltpu.VMEM),
        scratch_shapes=[
            pltpu.VMEM((128, BINS), bf16),
            pltpu.VMEM((128, BINS), bf16),
            pltpu.VMEM((384, 128), f32),
            pltpu.VMEM((384, 128), f32),
            pltpu.VMEM((16, 128), i32),
            pltpu.SMEM((16, 128), i32),
            pltpu.SMEM((2,), i32),
            pltpu.VMEM((8, BINS), f32),
            pltpu.VMEM((N_DET, 8, BINS), f32),
            pltpu.VMEM((N_TM, 4, BINS), bf16),
            pltpu.VMEM((N_TM, 4, BINS), bf16),
            pltpu.VMEM((CHUNKS, 256, 256), bf16),
            pltpu.VMEM((CHUNKS, 256, BINS), f32),
            pltpu.VMEM((CHUNKS, 256, BINS), f32),
            pltpu.VMEM((N_ZH, TILES_SUM, 8, BINS), f32),
            pltpu.VMEM((8, BINS), f32),
            pltpu.VMEM((N_ZH, 8, BINS), f32),
            pltpu.VMEM((32, BINS), f32),
            pltpu.VMEM((N_XYK, 1, BINS), f32),
            pltpu.VMEM((N_XYK, 1, BINS), f32),
            dma((6,)), dma, dma, dma((3,)), dma((3,)), dma, dma, dma, dma, dma, dma,
            pltpu.SemaphoreType.REGULAR, pltpu.SemaphoreType.REGULAR,
        ],
        compiler_params=pltpu.CompilerParams(
            collective_id=0, has_side_effects=True, vmem_limit_bytes=60 * 1024 * 1024
        ),
        name="radiometer",
    )(
        spectra.reshape(128, BINS),
        valid,
        lags.reshape(384, 128),
        drift.reshape(384, 128),
        table,
    )
    return out.reshape(BINS)[:PIX_OWN]


def solution(mesh):
    placed = (P("det", "tm", None, None, None), P("tm"), P(), P(), P())
    return jax.shard_map(
        shards, mesh=mesh, in_specs=placed, out_specs=P(("det", "tm")), check_vma=False
    )
```

```python
import math

import jax
import jax.numpy as jnp
from jax import lax
from jax.experimental import pallas as pl
from jax.experimental.pallas import tpu as pltpu
from jax.sharding import PartitionSpec as P

MESH = pl.DeviceIdType.MESH

N_DET = 4
N_TM = 128
N_Z = 8
N_XY = 16
N_ZH = 16
N_XYK = 32
BINS = 128
BANDS = 32
TILES_OWN = 3
TILES_SUM = 6
PIX_OWN = 96
CHUNKS = 8

SIN = [(-1.0) ** n * (2 * math.pi) ** (2 * n + 1) / math.factorial(2 * n + 1) for n in range(6)]
COS = [(-1.0) ** n * (2 * math.pi) ** (2 * n) / math.factorial(2 * n) for n in range(7)]


def horner(coefficients, x):
    total = jnp.full_like(x, coefficients[-1])
    for c in coefficients[-2::-1]:
        total = total * x + c
    return total


def cos_sin(turns):
    half = jnp.floor(turns * 2.0 + 0.5)
    r = turns - half * 0.5
    sign = 1.0 - 2.0 * (half - 2.0 * jnp.floor(half * 0.5))
    square = r * r
    return sign * horner(COS, square), sign * r * horner(SIN, square)


def iota(shape, dim):
    return lax.broadcasted_iota(jnp.int32, shape, dim)


def kernel(
    spec_hbm, valid_hbm, lags_hbm, drift_hbm, table_hbm, out_ref,
    own_v, other_v, lags_v, drift_v, table_v, table_s, valid_s,
    squares, squares_all, send2, recv2,
    kmat, rot_cos, rot_sin, masks, part, parts, folded, send4, recv4,
    local_sem, hl_send, hl_recv, sq_send, sq_recv,
    s2_send, s2_recv, s3_send, s3_recv, s4_send, s4_recv, plane_sem, space_sem,
):
    det = lax.axis_index("det")
    tm = lax.axis_index("tm")
    div, rem = lax.div, lax.rem
    k, h = div(det, 2), rem(det, 2)
    z, xy = div(tm, N_XY), rem(tm, N_XY)
    x, y = div(xy, 4), rem(xy, 4)
    yk = y * 2 + k
    zh = z * 2 + h
    xyk = xy * 2 + k

    def z_peer(r):
        return (det, rem(z + r, N_Z) * N_XY + xy)

    def x_peer(r):
        return (det, z * N_XY + rem(x + r, 4) * 4 + y)

    def y_peer(r):
        p = rem(yk + r, 8)
        return (rem(p, 2) * 2 + h, z * N_XY + x * 4 + div(p, 2))

    def zh_peer(r):
        p = rem(zh + r, N_ZH)
        return (k * 2 + rem(p, 2), div(p, 2) * N_XY + xy)

    def xyk_peer(r):
        p = rem(xyk + r, N_XYK)
        return (rem(p, 2) * 2 + h, z * N_XY + div(p, 2))

    step = 2 * k - 1

    def chip_at(distance):
        chip = rem(yk + step * distance + 8, 8)
        return rem(chip, 2) * 2 + h, div(chip, 2)

    sent_to = [chip_at(j) for j in range(4)]
    core_peer = (k * 2 + 1 - h, tm)
    across_peer = (3 - det, tm)

    barrier = pltpu.get_barrier_semaphore()

    def tell(semaphore, peer):
        pl.semaphore_signal(semaphore, inc=1, device_id=peer, device_id_type=MESH)

    @pl.loop(1, N_Z)
    def _(r):
        tell(barrier, z_peer(r))

    @pl.loop(1, 8)
    def _(r):
        tell(barrier, y_peer(r))

    @pl.loop(1, 4)
    def _(r):
        tell(barrier, x_peer(r))

    tell(barrier, core_peer)
    tell(barrier, across_peer)

    loads = [
        pltpu.make_async_copy(src, dst, local_sem.at[n])
        for n, (src, dst) in enumerate(
            [
                (spec_hbm, own_v), (table_hbm, table_s), (table_hbm, table_v),
                (valid_hbm, valid_s), (lags_hbm, lags_v), (drift_hbm, drift_v),
            ]
        )
    ]
    for load in loads:
        load.start()
    loads[0].wait()

    own = own_v[...].astype(jnp.float32)
    sq = own * own
    row8 = iota((8, BINS), 0)
    seg0 = jnp.sum(sq[:64], axis=0, keepdims=True)
    seg1 = jnp.sum(sq[64:], axis=0, keepdims=True)
    sums = jnp.where(row8 == 0, seg0, jnp.where(row8 == 1, seg1, 0.0))
    squares[...] = sums
    squares_all[det] = sums

    for load in loads[1:]:
        load.wait()

    bands = table_v[...].astype(jnp.float32)
    target = iota((4 * N_TM, BINS), 0)
    row = iota((4 * N_XY, BINS), 0)
    chip = (yk + step * (row // 4 % 4) + 8) % 8
    at = 32 * (row // 16) + 8 * (chip // 2) + 2 * (chip % 2) + 4 * h
    wanted = iota((4 * N_XY, BINS), 1) == at
    picks = []
    for dz in range(N_Z):
        column = jnp.where(wanted, bands[2 * dz : 2 * dz + 1], 0.0)
        picks.append(jnp.sum(column, axis=1, keepdims=True))
    pick = (jnp.concatenate(picks, axis=0) - (BANDS * h).astype(jnp.float32)) * 2.0
    segment = (target[:, 0:1] // 2 % 2).astype(jnp.float32) * 64.0
    is_imag = target[:, 0:1] % 2
    source = iota((4 * N_TM, BINS), 1).astype(jnp.float32)
    chosen = jnp.where(source == pick + segment, 1.0, 0.0)
    pick_real = jnp.where(is_imag == 0, chosen, 0.0).astype(jnp.bfloat16)
    pick_imag = jnp.where(is_imag == 1, chosen, 0.0).astype(jnp.bfloat16)
    pick = jnp.concatenate([pick_real, pick_imag], axis=1)

    pl.semaphore_wait(barrier, 7 + 7 + 3 + 2)

    @pl.loop(1, 4)
    def _(r):
        tell(plane_sem, x_peer(r))

    tell(plane_sem, core_peer)

    hl = pltpu.make_async_remote_copy(
        src_ref=own_v, dst_ref=other_v, send_sem=hl_send, recv_sem=hl_recv,
        device_id=(rem(det + 2, N_DET), tm), device_id_type=MESH,
    )
    hl.start()
    sq_copies = [
        pltpu.make_async_remote_copy(
            src_ref=squares, dst_ref=squares_all.at[det],
            send_sem=sq_send.at[r - 1], recv_sem=sq_recv.at[r - 1],
            device_id=(rem(det + r, N_DET), tm), device_id_type=MESH,
        )
        for r in range(1, N_DET)
    ]
    for copy in sq_copies:
        copy.start()

    pl.semaphore_wait(plane_sem, 4)

    for distance in (1, 3, -2):
        d, chip_y = chip_at(distance)
        tell(space_sem, (d, z * N_XY + x * 4 + chip_y))

    hl.wait_recv()
    other = other_v[...].astype(jnp.float32)
    own_up = pltpu.roll(own, BINS - 1, 0)
    other_up = pltpu.roll(other, BINS - 1, 0)
    sign = (1 - 2 * k).astype(jnp.float32)
    cross_real = own * other + own_up * other_up
    cross_imag = (own * other_up - own_up * other) * sign
    for copy in sq_copies:
        copy.wait_recv()
    total = lambda a: jnp.sum(a, axis=1, keepdims=True) / 8192.0 + 1e-06
    power_h = total(squares_all[0] + squares_all[1])
    power_l = total(squares_all[2] + squares_all[3])
    flags = jnp.where(iota((8, 1), 0) == 0, valid_s[0], valid_s[1]).astype(jnp.float32)
    weight = flags / (power_h * power_l)
    weights = jnp.where(iota((BINS, 1), 0) < 64, weight[0:1], weight[1:2])
    cross = jnp.concatenate([cross_real * weights, cross_imag * weights], axis=0)
    rows = jnp.dot(pick, cross.astype(jnp.bfloat16), preferred_element_type=jnp.float32)
    send2.reshape(4 * N_TM, BINS)[...] = rows.astype(jnp.bfloat16)

    zx = z * 4 + x

    def stage2(to_zx, j):
        d, chip_y = sent_to[j]
        return pltpu.make_async_remote_copy(
            src_ref=send2.at[4 * to_zx + j], dst_ref=recv2.at[tm],
            send_sem=s2_send, recv_sem=s2_recv,
            device_id=(d, 4 * to_zx + chip_y), device_id_type=MESH,
        )

    pl.semaphore_wait(space_sem, 3)

    for j in range(1, 4):
        stage2(zx, j).start()

    @pl.loop(1, 32)
    def _(r):
        to_zx = rem(zx + r, 32)
        for j in range(4):
            stage2(to_zx, j).start()

    recv2[tm] = send2[4 * zx]

    g = table_s[2 * z, 8 * xy + 4 * h + 2 * k]
    g_f = g.astype(jnp.float32)
    first = [table_s[2 * z + 1, 8 * xy + 4 * h + 2 * k + n] for n in range(2)]
    col16 = iota((16, BINS), 0)
    col8 = iota((8, BINS), 0)

    @pl.loop(0, CHUNKS)
    def _(ch):
        tile = jnp.where(ch < 4, first[0], first[1])
        lag = lags_v[pl.ds(4 * tile + ch % 4, 1), :]
        ca, sa = cos_sin((g * BINS + 16 * col8).astype(jnp.float32) * lag)
        cb, sb = cos_sin(col16.astype(jnp.float32) * lag)
        for a in range(8):
            c1, s1 = ca[a : a + 1], sa[a : a + 1]
            cosine = (c1 * cb - s1 * sb).astype(jnp.bfloat16)
            sine = (s1 * cb + c1 * sb).astype(jnp.bfloat16)
            kmat[ch, 16 * a : 16 * a + 16, 0:BINS] = cosine
            kmat[ch, 16 * a : 16 * a + 16, BINS:] = -sine
            kmat[ch, BINS + 16 * a : BINS + 16 * a + 16, 0:BINS] = sine
            kmat[ch, BINS + 16 * a : BINS + 16 * a + 16, BINS:] = cosine

    time_a = (16 * col16).astype(jnp.float32) - 127.5
    time_b = (2 * (col16 % 8) + col16 // 8).astype(jnp.float32)
    scale = (g_f + 0.5) * (1.0 / (64 * 256))

    @pl.loop(0, CHUNKS)
    def _(ch):
        tile = jnp.where(ch < 4, first[0], first[1])
        rate = drift_v[pl.ds(4 * tile + ch % 4, 1), :] * scale
        ca, sa = cos_sin(time_a * rate)
        cb, sb = cos_sin(time_b * rate)
        for a in range(16):
            c1, s1 = ca[a : a + 1], sa[a : a + 1]
            cosine = c1 * cb - s1 * sb
            sine = s1 * cb + c1 * sb
            for s in range(2):
                at = s * N_TM + 8 * a
                rot_cos[ch, at : at + 8, :] = cosine[8 * s : 8 * s + 8]
                rot_sin[ch, at : at + 8, :] = sine[8 * s : 8 * s + 8]

    @pl.loop(0, N_ZH)
    def _(p):
        at = 8 * xy + 4 * (p % 2) + 2 * k
        t0 = table_s[2 * (p // 2) + 1, at]
        t1 = table_s[2 * (p // 2) + 1, at + 1]
        tiles = jnp.where(row8 < 4, t0, t1)
        for j in range(TILES_SUM):
            tile = 24 * (j // 3 * 2 + h) + 3 * z + j % 3
            masks[p, j] = jnp.where(tiles == tile, 1.0, 0.0)

    o, n = iota((256, 512), 0), iota((256, 512), 1)
    want = 4 * (o % N_TM) + 2 * (o // N_TM)
    perms = [
        jnp.where(n == want + c, 1.0, 0.0).astype(jnp.bfloat16) for c in range(2)
    ]

    pltpu.make_async_copy(
        recv2.at[pl.ds(0, N_TM - 1)], recv2.at[pl.ds(0, N_TM - 1)], s2_recv
    ).wait()

    got = recv2.reshape(4 * N_TM, BINS)[...]
    slab = jnp.concatenate(
        [jnp.dot(p, got, preferred_element_type=jnp.float32) for p in perms], axis=1
    ).astype(jnp.bfloat16)

    for ch in range(CHUNKS):
        product = jnp.dot(slab, kmat[ch], preferred_element_type=jnp.float32)
        turned = rot_cos[ch] * product[:, :BINS] - rot_sin[ch] * product[:, BINS:]
        part[ch : ch + 1, :] = jnp.sum(turned, axis=0, keepdims=True)

    def stage3(r):
        return pltpu.make_async_remote_copy(
            src_ref=part, dst_ref=parts.at[zh],
            send_sem=s3_send, recv_sem=s3_recv,
            device_id=zh_peer(r), device_id_type=MESH,
        )

    @pl.loop(1, N_ZH)
    def _(r):
        stage3(r).start()

    parts[zh] = part[...]
    pltpu.make_async_copy(
        parts.at[pl.ds(0, N_ZH - 1)], parts.at[pl.ds(0, N_ZH - 1)], s3_recv
    ).wait()

    sums = [jnp.zeros((8, BINS), jnp.float32) for _ in range(TILES_SUM)]
    for p in range(N_ZH):
        terms = parts[p]
        for j in range(TILES_SUM):
            sums[j] += terms * masks[p, j]
    for j in range(TILES_SUM):
        at = 16 * (j // 3) + 4 * (j % 3)
        folded[at : at + 4, :] = sums[j][0:4] + sums[j][4:8]
    lane4 = iota((4, BINS), 1)
    for q in range(2):
        rows = [folded[pl.ds(16 * q + i, 4, stride=3), :] for i in range(3)]
        for j in range(4):
            at, shift = 96 * j // BINS, 96 * j % BINS
            low = pltpu.roll(rows[at], BINS - shift, 1) if shift else rows[at]
            if BINS - shift < PIX_OWN:
                high = pltpu.roll(rows[at + 1], BINS - shift, 1)
                low = jnp.where(lane4 < BINS - shift, low, high)
            for i in range(4):
                send4[(4 * i + j) * 2 + q] = low[i : i + 1]

    def stage4(r):
        return pltpu.make_async_remote_copy(
            src_ref=send4.at[rem(xyk + r, N_XYK)], dst_ref=recv4.at[xyk],
            send_sem=s4_send, recv_sem=s4_recv,
            device_id=xyk_peer(r), device_id_type=MESH,
        )

    @pl.loop(1, N_XYK)
    def _(r):
        stage4(r).start()

    recv4[xyk] = send4[xyk]
    hl.wait_send()
    for copy in sq_copies:
        copy.wait_send()
    pltpu.make_async_copy(
        send2.at[pl.ds(0, N_TM - 1)], send2.at[pl.ds(0, N_TM - 1)], s2_send
    ).wait()
    pltpu.make_async_copy(
        parts.at[pl.ds(0, N_ZH - 1)], parts.at[pl.ds(0, N_ZH - 1)], s3_send
    ).wait()
    pltpu.make_async_copy(
        send4.at[pl.ds(0, N_XYK - 1)], send4.at[pl.ds(0, N_XYK - 1)], s4_send
    ).wait()
    pltpu.make_async_copy(
        recv4.at[pl.ds(0, N_XYK - 1)], recv4.at[pl.ds(0, N_XYK - 1)], s4_recv
    ).wait()
    pieces = recv4.reshape(N_XYK, BINS)[...]
    total = jnp.sum(pieces, axis=0, keepdims=True)
    out_ref[...] = total * (1.0 / math.sqrt(256 * BINS))


def shards(spectra, valid, lags, drift, block_table):
    f32, bf16, i32 = jnp.float32, jnp.bfloat16, jnp.int32
    table = block_table.reshape(8, 128, 2).transpose(0, 2, 1).reshape(16, 128)
    dma = pltpu.SemaphoreType.DMA
    out = pl.pallas_call(
        kernel,
        out_shape=pltpu.VMEM((1, BINS), f32),
        in_specs=[pl.BlockSpec(memory_space=pltpu.HBM)] * 5,
        out_specs=pl.BlockSpec(memory_space=pltpu.VMEM),
        scratch_shapes=[
            pltpu.VMEM((128, BINS), bf16),
            pltpu.VMEM((128, BINS), bf16),
            pltpu.VMEM((384, 128), f32),
            pltpu.VMEM((384, 128), f32),
            pltpu.VMEM((16, 128), i32),
            pltpu.SMEM((16, 128), i32),
            pltpu.SMEM((2,), i32),
            pltpu.VMEM((8, BINS), f32),
            pltpu.VMEM((N_DET, 8, BINS), f32),
            pltpu.VMEM((N_TM, 4, BINS), bf16),
            pltpu.VMEM((N_TM, 4, BINS), bf16),
            pltpu.VMEM((CHUNKS, 256, 256), bf16),
            pltpu.VMEM((CHUNKS, 256, BINS), f32),
            pltpu.VMEM((CHUNKS, 256, BINS), f32),
            pltpu.VMEM((N_ZH, TILES_SUM, 8, BINS), f32),
            pltpu.VMEM((8, BINS), f32),
            pltpu.VMEM((N_ZH, 8, BINS), f32),
            pltpu.VMEM((32, BINS), f32),
            pltpu.VMEM((N_XYK, 1, BINS), f32),
            pltpu.VMEM((N_XYK, 1, BINS), f32),
            dma((6,)), dma, dma, dma((3,)), dma((3,)), dma, dma, dma, dma, dma, dma,
            pltpu.SemaphoreType.REGULAR, pltpu.SemaphoreType.REGULAR,
        ],
        compiler_params=pltpu.CompilerParams(
            collective_id=0, has_side_effects=True, vmem_limit_bytes=60 * 1024 * 1024
        ),
        name="radiometer",
    )(
        spectra.reshape(128, BINS),
        valid,
        lags.reshape(384, 128),
        drift.reshape(384, 128),
        table,
    )
    return out.reshape(BINS)[:PIX_OWN]


def solution(mesh):
    placed = (P("det", "tm", None, None, None), P("tm"), P(), P(), P())
    return jax.shard_map(
        shards, mesh=mesh, in_specs=placed, out_specs=P(("det", "tm")), check_vma=False
    )
```

```python
import math

import jax
import jax.numpy as jnp
from jax import lax
from jax.experimental import pallas as pl
from jax.experimental.pallas import tpu as pltpu
from jax.sharding import PartitionSpec as P

MESH = pl.DeviceIdType.MESH

N_DET = 4
N_TM = 128
N_Z = 8
N_XY = 16
N_ZH = 16
N_XYK = 32
BINS = 128
BANDS = 32
TILES_OWN = 3
TILES_SUM = 6
PIX_OWN = 96
CHUNKS = 8

SIN = [(-1.0) ** n * (2 * math.pi) ** (2 * n + 1) / math.factorial(2 * n + 1) for n in range(6)]
COS = [(-1.0) ** n * (2 * math.pi) ** (2 * n) / math.factorial(2 * n) for n in range(7)]


def horner(coefficients, x):
    total = jnp.full_like(x, coefficients[-1])
    for c in coefficients[-2::-1]:
        total = total * x + c
    return total


def cos_sin(turns):
    half = jnp.floor(turns * 2.0 + 0.5)
    r = turns - half * 0.5
    sign = 1.0 - 2.0 * (half - 2.0 * jnp.floor(half * 0.5))
    square = r * r
    return sign * horner(COS, square), sign * r * horner(SIN, square)


def iota(shape, dim):
    return lax.broadcasted_iota(jnp.int32, shape, dim)


def kernel(
    spec_hbm, valid_hbm, lags_hbm, drift_hbm, table_hbm, out_ref,
    own_v, other_v, lags_v, drift_v, table_v, table_s, valid_s,
    squares, squares_all, send2, recv2,
    kmat, rot_cos, rot_sin, masks, part, parts, folded, send4, recv4,
    local_sem, hl_send, hl_recv, sq_send, sq_recv,
    s2_send, s2_recv, s3_send, s3_recv, s4_send, s4_recv, plane_sem, space_sem,
):
    det = lax.axis_index("det")
    tm = lax.axis_index("tm")
    k, h = det // 2, det % 2
    z, xy = tm // N_XY, tm % N_XY
    x, y = xy // 4, xy % 4
    yk = y * 2 + k
    zh = z * 2 + h
    xyk = xy * 2 + k

    def z_peer(r):
        return (det, (z + r) % N_Z * N_XY + xy)

    def x_peer(r):
        return (det, z * N_XY + (x + r) % 4 * 4 + y)

    def y_peer(r):
        p = (yk + r) % 8
        return (p % 2 * 2 + h, z * N_XY + x * 4 + p // 2)

    def zh_peer(r):
        p = (zh + r) % N_ZH
        return (k * 2 + p % 2, p // 2 * N_XY + xy)

    def xyk_peer(r):
        p = (xyk + r) % N_XYK
        return (p % 2 * 2 + h, z * N_XY + p // 2)

    step = 2 * k - 1

    def chip_at(distance):
        chip = (yk + step * distance + 8) % 8
        return chip % 2 * 2 + h, chip // 2

    sent_to = [chip_at(j) for j in range(4)]
    core_peer = (k * 2 + 1 - h, tm)
    across_peer = (3 - det, tm)

    barrier = pltpu.get_barrier_semaphore()

    def tell(semaphore, peer):
        pl.semaphore_signal(semaphore, inc=1, device_id=peer, device_id_type=MESH)

    @pl.loop(1, N_Z)
    def _(r):
        tell(barrier, z_peer(r))

    @pl.loop(1, 8)
    def _(r):
        tell(barrier, y_peer(r))

    @pl.loop(1, 4)
    def _(r):
        tell(barrier, x_peer(r))

    tell(barrier, core_peer)
    tell(barrier, across_peer)

    loads = [
        pltpu.make_async_copy(src, dst, local_sem.at[n])
        for n, (src, dst) in enumerate(
            [
                (spec_hbm, own_v), (table_hbm, table_s), (table_hbm, table_v),
                (valid_hbm, valid_s), (lags_hbm, lags_v), (drift_hbm, drift_v),
            ]
        )
    ]
    for load in loads:
        load.start()
    pl.semaphore_wait(barrier, 7 + 7 + 3 + 2)

    @pl.loop(1, 4)
    def _(r):
        tell(plane_sem, x_peer(r))

    tell(plane_sem, core_peer)

    hl = pltpu.make_async_remote_copy(
        src_ref=spec_hbm, dst_ref=other_v, send_sem=hl_send, recv_sem=hl_recv,
        device_id=((det + 2) % N_DET, tm), device_id_type=MESH,
    )
    hl.start()
    loads[0].wait()

    own = own_v[...].astype(jnp.float32)
    sq = own * own
    row8 = iota((8, BINS), 0)
    seg0 = jnp.sum(sq[:64], axis=0, keepdims=True)
    seg1 = jnp.sum(sq[64:], axis=0, keepdims=True)
    sums = jnp.where(row8 == 0, seg0, jnp.where(row8 == 1, seg1, 0.0))
    squares[...] = sums
    squares_all[det] = sums

    sq_copies = [
        pltpu.make_async_remote_copy(
            src_ref=squares, dst_ref=squares_all.at[det],
            send_sem=sq_send.at[r - 1], recv_sem=sq_recv.at[r - 1],
            device_id=((det + r) % N_DET, tm), device_id_type=MESH,
        )
        for r in range(1, N_DET)
    ]
    for copy in sq_copies:
        copy.start()

    pl.semaphore_wait(plane_sem, 4)

    for distance in (1, 3, -2):
        d, chip_y = chip_at(distance)
        tell(space_sem, (d, z * N_XY + x * 4 + chip_y))

    for load in loads[1:]:
        load.wait()

    bands = table_v[...].astype(jnp.float32)
    target = iota((4 * N_TM, BINS), 0)
    row = iota((4 * N_XY, BINS), 0)
    chip = (yk + step * (row // 4 % 4) + 8) % 8
    at = 32 * (row // 16) + 8 * (chip // 2) + 2 * (chip % 2) + 4 * h
    wanted = iota((4 * N_XY, BINS), 1) == at
    picks = []
    for dz in range(N_Z):
        column = jnp.where(wanted, bands[2 * dz : 2 * dz + 1], 0.0)
        picks.append(jnp.sum(column, axis=1, keepdims=True))
    pick = (jnp.concatenate(picks, axis=0) - (BANDS * h).astype(jnp.float32)) * 2.0
    segment = (target[:, 0:1] // 2 % 2).astype(jnp.float32) * 64.0
    is_imag = target[:, 0:1] % 2
    source = iota((4 * N_TM, BINS), 1).astype(jnp.float32)
    chosen = jnp.where(source == pick + segment, 1.0, 0.0)
    pick_real = jnp.where(is_imag == 0, chosen, 0.0).astype(jnp.bfloat16)
    pick_imag = jnp.where(is_imag == 1, chosen, 0.0).astype(jnp.bfloat16)
    pick = jnp.concatenate([pick_real, pick_imag], axis=1)

    hl.wait_recv()
    other = other_v[...].astype(jnp.float32)
    own_up = pltpu.roll(own, BINS - 1, 0)
    other_up = pltpu.roll(other, BINS - 1, 0)
    sign = (1 - 2 * k).astype(jnp.float32)
    cross_real = own * other + own_up * other_up
    cross_imag = (own * other_up - own_up * other) * sign
    for copy in sq_copies:
        copy.wait_recv()
    total = lambda a: jnp.sum(a, axis=1, keepdims=True) / 8192.0 + 1e-06
    power_h = total(squares_all[0] + squares_all[1])
    power_l = total(squares_all[2] + squares_all[3])
    flags = jnp.where(iota((8, 1), 0) == 0, valid_s[0], valid_s[1]).astype(jnp.float32)
    weight = flags / (power_h * power_l)
    weights = jnp.where(iota((BINS, 1), 0) < 64, weight[0:1], weight[1:2])
    cross = jnp.concatenate([cross_real * weights, cross_imag * weights], axis=0)
    rows = jnp.dot(pick, cross.astype(jnp.bfloat16), preferred_element_type=jnp.float32)
    send2.reshape(4 * N_TM, BINS)[...] = rows.astype(jnp.bfloat16)

    zx = z * 4 + x

    def stage2(to_zx, j):
        d, chip_y = sent_to[j]
        return pltpu.make_async_remote_copy(
            src_ref=send2.at[4 * to_zx + j], dst_ref=recv2.at[tm],
            send_sem=s2_send, recv_sem=s2_recv,
            device_id=(d, 4 * to_zx + chip_y), device_id_type=MESH,
        )

    pl.semaphore_wait(space_sem, 3)

    for j in range(1, 4):
        stage2(zx, j).start()

    @pl.loop(1, 32)
    def _(r):
        for j in range(4):
            stage2((zx + r) % 32, j).start()

    recv2[tm] = send2[4 * zx]

    g = table_s[2 * z, 8 * xy + 4 * h + 2 * k]
    g_f = g.astype(jnp.float32)
    first = [table_s[2 * z + 1, 8 * xy + 4 * h + 2 * k + n] for n in range(2)]
    col16 = iota((16, BINS), 0)
    col8 = iota((8, BINS), 0)

    @pl.loop(0, CHUNKS)
    def _(ch):
        tile = jnp.where(ch < 4, first[0], first[1])
        lag = lags_v[pl.ds(4 * tile + ch % 4, 1), :]
        ca, sa = cos_sin((g * BINS + 16 * col8).astype(jnp.float32) * lag)
        cb, sb = cos_sin(col16.astype(jnp.float32) * lag)
        for a in range(8):
            c1, s1 = ca[a : a + 1], sa[a : a + 1]
            cosine = (c1 * cb - s1 * sb).astype(jnp.bfloat16)
            sine = (s1 * cb + c1 * sb).astype(jnp.bfloat16)
            kmat[ch, 16 * a : 16 * a + 16, 0:BINS] = cosine
            kmat[ch, 16 * a : 16 * a + 16, BINS:] = -sine
            kmat[ch, BINS + 16 * a : BINS + 16 * a + 16, 0:BINS] = sine
            kmat[ch, BINS + 16 * a : BINS + 16 * a + 16, BINS:] = cosine

    time_a = (16 * col16).astype(jnp.float32) - 127.5
    time_b = (2 * (col16 % 8) + col16 // 8).astype(jnp.float32)
    scale = (g_f + 0.5) * (1.0 / (64 * 256))

    @pl.loop(0, CHUNKS)
    def _(ch):
        tile = jnp.where(ch < 4, first[0], first[1])
        rate = drift_v[pl.ds(4 * tile + ch % 4, 1), :] * scale
        ca, sa = cos_sin(time_a * rate)
        cb, sb = cos_sin(time_b * rate)
        for a in range(16):
            c1, s1 = ca[a : a + 1], sa[a : a + 1]
            cosine = c1 * cb - s1 * sb
            sine = s1 * cb + c1 * sb
            for s in range(2):
                at = s * N_TM + 8 * a
                rot_cos[ch, at : at + 8, :] = cosine[8 * s : 8 * s + 8]
                rot_sin[ch, at : at + 8, :] = sine[8 * s : 8 * s + 8]

    @pl.loop(0, N_ZH)
    def _(p):
        at = 8 * xy + 4 * (p % 2) + 2 * k
        t0 = table_s[2 * (p // 2) + 1, at]
        t1 = table_s[2 * (p // 2) + 1, at + 1]
        tiles = jnp.where(row8 < 4, t0, t1)
        for j in range(TILES_SUM):
            tile = 24 * (j // 3 * 2 + h) + 3 * z + j % 3
            masks[p, j] = jnp.where(tiles == tile, 1.0, 0.0)

    o, n = iota((256, 512), 0), iota((256, 512), 1)
    want = 4 * (o % N_TM) + 2 * (o // N_TM)
    perms = [
        jnp.where(n == want + c, 1.0, 0.0).astype(jnp.bfloat16) for c in range(2)
    ]

    pltpu.make_async_copy(
        recv2.at[pl.ds(0, N_TM - 1)], recv2.at[pl.ds(0, N_TM - 1)], s2_recv
    ).wait()

    got = recv2.reshape(4 * N_TM, BINS)[...]
    slab = jnp.concatenate(
        [jnp.dot(p, got, preferred_element_type=jnp.float32) for p in perms], axis=1
    ).astype(jnp.bfloat16)

    for ch in range(CHUNKS):
        product = jnp.dot(slab, kmat[ch], preferred_element_type=jnp.float32)
        turned = rot_cos[ch] * product[:, :BINS] - rot_sin[ch] * product[:, BINS:]
        part[ch : ch + 1, :] = jnp.sum(turned, axis=0, keepdims=True)

    def stage3(r):
        return pltpu.make_async_remote_copy(
            src_ref=part, dst_ref=parts.at[zh],
            send_sem=s3_send, recv_sem=s3_recv,
            device_id=zh_peer(r), device_id_type=MESH,
        )

    @pl.loop(1, N_ZH)
    def _(r):
        stage3(r).start()

    parts[zh] = part[...]
    pltpu.make_async_copy(
        parts.at[pl.ds(0, N_ZH - 1)], parts.at[pl.ds(0, N_ZH - 1)], s3_recv
    ).wait()

    sums = [jnp.zeros((8, BINS), jnp.float32) for _ in range(TILES_SUM)]
    for p in range(N_ZH):
        terms = parts[p]
        for j in range(TILES_SUM):
            sums[j] += terms * masks[p, j]
    for j in range(TILES_SUM):
        at = 16 * (j // 3) + 4 * (j % 3)
        folded[at : at + 4, :] = sums[j][0:4] + sums[j][4:8]
    lane4 = iota((4, BINS), 1)
    for q in range(2):
        rows = [folded[pl.ds(16 * q + i, 4, stride=3), :] for i in range(3)]
        for j in range(4):
            at, shift = 96 * j // BINS, 96 * j % BINS
            low = pltpu.roll(rows[at], BINS - shift, 1) if shift else rows[at]
            if BINS - shift < PIX_OWN:
                high = pltpu.roll(rows[at + 1], BINS - shift, 1)
                low = jnp.where(lane4 < BINS - shift, low, high)
            for i in range(4):
                send4[(4 * i + j) * 2 + q] = low[i : i + 1]

    def stage4(r):
        return pltpu.make_async_remote_copy(
            src_ref=send4.at[(xyk + r) % N_XYK], dst_ref=recv4.at[xyk],
            send_sem=s4_send, recv_sem=s4_recv,
            device_id=xyk_peer(r), device_id_type=MESH,
        )

    @pl.loop(1, N_XYK)
    def _(r):
        stage4(r).start()

    recv4[xyk] = send4[xyk]
    hl.wait_send()
    for copy in sq_copies:
        copy.wait_send()
    pltpu.make_async_copy(
        send2.at[pl.ds(0, N_TM - 1)], send2.at[pl.ds(0, N_TM - 1)], s2_send
    ).wait()
    pltpu.make_async_copy(
        parts.at[pl.ds(0, N_ZH - 1)], parts.at[pl.ds(0, N_ZH - 1)], s3_send
    ).wait()
    pltpu.make_async_copy(
        send4.at[pl.ds(0, N_XYK - 1)], send4.at[pl.ds(0, N_XYK - 1)], s4_send
    ).wait()
    pltpu.make_async_copy(
        recv4.at[pl.ds(0, N_XYK - 1)], recv4.at[pl.ds(0, N_XYK - 1)], s4_recv
    ).wait()
    total = recv4[0]
    for q in range(1, N_XYK):
        total += recv4[q]
    out_ref[...] = total * (1.0 / math.sqrt(256 * BINS))


def shards(spectra, valid, lags, drift, block_table):
    f32, bf16, i32 = jnp.float32, jnp.bfloat16, jnp.int32
    table = block_table.reshape(8, 128, 2).transpose(0, 2, 1).reshape(16, 128)
    dma = pltpu.SemaphoreType.DMA
    out = pl.pallas_call(
        kernel,
        out_shape=pltpu.VMEM((1, BINS), f32),
        in_specs=[pl.BlockSpec(memory_space=pltpu.HBM)] * 5,
        out_specs=pl.BlockSpec(memory_space=pltpu.VMEM),
        scratch_shapes=[
            pltpu.VMEM((128, BINS), bf16),
            pltpu.VMEM((128, BINS), bf16),
            pltpu.VMEM((384, 128), f32),
            pltpu.VMEM((384, 128), f32),
            pltpu.VMEM((16, 128), i32),
            pltpu.SMEM((16, 128), i32),
            pltpu.SMEM((2,), i32),
            pltpu.VMEM((8, BINS), f32),
            pltpu.VMEM((N_DET, 8, BINS), f32),
            pltpu.VMEM((N_TM, 4, BINS), bf16),
            pltpu.VMEM((N_TM, 4, BINS), bf16),
            pltpu.VMEM((CHUNKS, 256, 256), bf16),
            pltpu.VMEM((CHUNKS, 256, BINS), f32),
            pltpu.VMEM((CHUNKS, 256, BINS), f32),
            pltpu.VMEM((N_ZH, TILES_SUM, 8, BINS), f32),
            pltpu.VMEM((8, BINS), f32),
            pltpu.VMEM((N_ZH, 8, BINS), f32),
            pltpu.VMEM((32, BINS), f32),
            pltpu.VMEM((N_XYK, 1, BINS), f32),
            pltpu.VMEM((N_XYK, 1, BINS), f32),
            dma((6,)), dma, dma, dma((3,)), dma((3,)), dma, dma, dma, dma, dma, dma,
            pltpu.SemaphoreType.REGULAR, pltpu.SemaphoreType.REGULAR,
        ],
        compiler_params=pltpu.CompilerParams(
            collective_id=0, has_side_effects=True, vmem_limit_bytes=60 * 1024 * 1024
        ),
        name="radiometer",
    )(
        spectra.reshape(128, BINS),
        valid,
        lags.reshape(384, 128),
        drift.reshape(384, 128),
        table,
    )
    return out.reshape(BINS)[:PIX_OWN]


def solution(mesh):
    placed = (P("det", "tm", None, None, None), P("tm"), P(), P(), P())
    return jax.shard_map(
        shards, mesh=mesh, in_specs=placed, out_specs=P(("det", "tm")), check_vma=False
    )
```

```python
import math

import jax
import jax.numpy as jnp
from jax import lax
from jax.experimental import pallas as pl
from jax.experimental.pallas import tpu as pltpu
from jax.sharding import PartitionSpec as P

MESH = pl.DeviceIdType.MESH

N_DET = 4
N_TM = 128
N_Z = 8
N_XY = 16
N_ZH = 16
N_XYK = 32
BINS = 128
BANDS = 32
TILES_OWN = 3
TILES_SUM = 6
PIX_OWN = 96
CHUNKS = 8

SIN = [(-1.0) ** n * (2 * math.pi) ** (2 * n + 1) / math.factorial(2 * n + 1) for n in range(6)]
COS = [(-1.0) ** n * (2 * math.pi) ** (2 * n) / math.factorial(2 * n) for n in range(7)]


def horner(coefficients, x):
    total = jnp.full_like(x, coefficients[-1])
    for c in coefficients[-2::-1]:
        total = total * x + c
    return total


def cos_sin(turns):
    half = jnp.floor(turns * 2.0 + 0.5)
    r = turns - half * 0.5
    sign = 1.0 - 2.0 * (half - 2.0 * jnp.floor(half * 0.5))
    square = r * r
    return sign * horner(COS, square), sign * r * horner(SIN, square)


def iota(shape, dim):
    return lax.broadcasted_iota(jnp.int32, shape, dim)


def kernel(
    spec_hbm, valid_hbm, lags_hbm, drift_hbm, table_hbm, out_ref,
    own_v, other_v, lags_v, drift_v, table_v, table_s, valid_s,
    squares, squares_all, send2, recv2,
    kmat, rot_cos, rot_sin, masks, part, parts, folded, send4, recv4,
    local_sem, hl_send, hl_recv, sq_send, sq_recv,
    s2_send, s2_recv, s3_send, s3_recv, s4_send, s4_recv, plane_sem, space_sem,
):
    det = lax.axis_index("det")
    tm = lax.axis_index("tm")
    div, rem = lax.div, lax.rem
    k, h = div(det, 2), rem(det, 2)
    z, xy = div(tm, N_XY), rem(tm, N_XY)
    x, y = div(xy, 4), rem(xy, 4)
    yk = y * 2 + k
    zh = z * 2 + h
    xyk = xy * 2 + k

    def z_peer(r):
        return (det, rem(z + r, N_Z) * N_XY + xy)

    def x_peer(r):
        return (det, z * N_XY + rem(x + r, 4) * 4 + y)

    def y_peer(r):
        p = rem(yk + r, 8)
        return (rem(p, 2) * 2 + h, z * N_XY + x * 4 + div(p, 2))

    def zh_peer(r):
        p = rem(zh + r, N_ZH)
        return (k * 2 + rem(p, 2), div(p, 2) * N_XY + xy)

    def xyk_peer(r):
        p = rem(xyk + r, N_XYK)
        return (rem(p, 2) * 2 + h, z * N_XY + div(p, 2))

    step = 2 * k - 1

    def chip_at(distance):
        chip = rem(yk + step * distance + 8, 8)
        return rem(chip, 2) * 2 + h, div(chip, 2)

    sent_to = [chip_at(j) for j in range(4)]
    core_peer = (k * 2 + 1 - h, tm)
    across_peer = (3 - det, tm)

    barrier = pltpu.get_barrier_semaphore()

    def tell(semaphore, peer):
        pl.semaphore_signal(semaphore, inc=1, device_id=peer, device_id_type=MESH)

    @pl.loop(1, N_Z)
    def _(r):
        tell(barrier, z_peer(r))

    @pl.loop(1, 8)
    def _(r):
        tell(barrier, y_peer(r))

    @pl.loop(1, 4)
    def _(r):
        tell(barrier, x_peer(r))

    tell(barrier, core_peer)
    tell(barrier, across_peer)

    loads = [
        pltpu.make_async_copy(src, dst, local_sem.at[n])
        for n, (src, dst) in enumerate(
            [
                (spec_hbm, own_v), (table_hbm, table_s), (table_hbm, table_v),
                (valid_hbm, valid_s), (lags_hbm, lags_v), (drift_hbm, drift_v),
            ]
        )
    ]
    for load in loads:
        load.start()
    loads[0].wait()

    own = own_v[...].astype(jnp.float32)
    sq = own * own
    row8 = iota((8, BINS), 0)
    seg0 = jnp.sum(sq[:64], axis=0, keepdims=True)
    seg1 = jnp.sum(sq[64:], axis=0, keepdims=True)
    sums = jnp.where(row8 == 0, seg0, jnp.where(row8 == 1, seg1, 0.0))
    squares[...] = sums
    squares_all[det] = sums

    for load in loads[1:]:
        load.wait()

    bands = table_v[...].astype(jnp.float32)
    target = iota((4 * N_TM, BINS), 0)
    row = iota((4 * N_XY, BINS), 0)
    chip = (yk + step * (row // 4 % 4) + 8) % 8
    at = 32 * (row // 16) + 8 * (chip // 2) + 2 * (chip % 2) + 4 * h
    wanted = iota((4 * N_XY, BINS), 1) == at
    picks = []
    for dz in range(N_Z):
        column = jnp.where(wanted, bands[2 * dz : 2 * dz + 1], 0.0)
        picks.append(jnp.sum(column, axis=1, keepdims=True))
    pick = (jnp.concatenate(picks, axis=0) - (BANDS * h).astype(jnp.float32)) * 2.0
    segment = (target[:, 0:1] // 2 % 2).astype(jnp.float32) * 64.0
    is_imag = target[:, 0:1] % 2
    source = iota((4 * N_TM, BINS), 1).astype(jnp.float32)
    chosen = jnp.where(source == pick + segment, 1.0, 0.0)
    pick_real = jnp.where(is_imag == 0, chosen, 0.0).astype(jnp.bfloat16)
    pick_imag = jnp.where(is_imag == 1, chosen, 0.0).astype(jnp.bfloat16)
    pick = jnp.concatenate([pick_real, pick_imag], axis=1)

    pl.semaphore_wait(barrier, 7 + 7 + 3 + 2)

    @pl.loop(1, 4)
    def _(r):
        tell(plane_sem, x_peer(r))

    tell(plane_sem, core_peer)

    hl = pltpu.make_async_remote_copy(
        src_ref=own_v, dst_ref=other_v, send_sem=hl_send, recv_sem=hl_recv,
        device_id=(rem(det + 2, N_DET), tm), device_id_type=MESH,
    )
    sq_copies = [
        pltpu.make_async_remote_copy(
            src_ref=squares, dst_ref=squares_all.at[det],
            send_sem=sq_send.at[r - 1], recv_sem=sq_recv.at[r - 1],
            device_id=(rem(det + r, N_DET), tm), device_id_type=MESH,
        )
        for r in range(1, N_DET)
    ]
    for copy in sq_copies:
        copy.start()
    hl.start()

    pl.semaphore_wait(plane_sem, 4)

    for distance in (1, 3, -2):
        d, chip_y = chip_at(distance)
        tell(space_sem, (d, z * N_XY + x * 4 + chip_y))

    for copy in sq_copies:
        copy.wait_recv()
    total = lambda a: jnp.sum(a, axis=1, keepdims=True) / 8192.0 + 1e-06
    power_h = total(squares_all[0] + squares_all[1])
    power_l = total(squares_all[2] + squares_all[3])
    flags = jnp.where(iota((8, 1), 0) == 0, valid_s[0], valid_s[1]).astype(jnp.float32)
    weight = flags / (power_h * power_l)
    weights = jnp.where(iota((BINS, 1), 0) < 64, weight[0:1], weight[1:2])

    hl.wait_recv()
    other = other_v[...].astype(jnp.float32)
    own_up = pltpu.roll(own, BINS - 1, 0)
    other_up = pltpu.roll(other, BINS - 1, 0)
    sign = (1 - 2 * k).astype(jnp.float32)
    cross_real = own * other + own_up * other_up
    cross_imag = (own * other_up - own_up * other) * sign
    cross = jnp.concatenate([cross_real * weights, cross_imag * weights], axis=0)
    rows = jnp.dot(pick, cross.astype(jnp.bfloat16), preferred_element_type=jnp.float32)
    send2.reshape(4 * N_TM, BINS)[...] = rows.astype(jnp.bfloat16)

    zx = z * 4 + x

    def stage2(to_zx, j):
        d, chip_y = sent_to[j]
        return pltpu.make_async_remote_copy(
            src_ref=send2.at[4 * to_zx + j], dst_ref=recv2.at[tm],
            send_sem=s2_send, recv_sem=s2_recv,
            device_id=(d, 4 * to_zx + chip_y), device_id_type=MESH,
        )

    pl.semaphore_wait(space_sem, 3)

    for j in range(1, 4):
        stage2(zx, j).start()

    @pl.loop(1, 32)
    def _(r):
        to_zx = rem(zx + r, 32)
        for j in range(4):
            stage2(to_zx, j).start()

    recv2[tm] = send2[4 * zx]

    g = table_s[2 * z, 8 * xy + 4 * h + 2 * k]
    g_f = g.astype(jnp.float32)
    first = [table_s[2 * z + 1, 8 * xy + 4 * h + 2 * k + n] for n in range(2)]
    col16 = iota((16, BINS), 0)
    col8 = iota((8, BINS), 0)

    @pl.loop(0, CHUNKS)
    def _(ch):
        tile = jnp.where(ch < 4, first[0], first[1])
        lag = lags_v[pl.ds(4 * tile + ch % 4, 1), :]
        ca, sa = cos_sin((g * BINS + 16 * col8).astype(jnp.float32) * lag)
        cb, sb = cos_sin(col16.astype(jnp.float32) * lag)
        for a in range(8):
            c1, s1 = ca[a : a + 1], sa[a : a + 1]
            cosine = (c1 * cb - s1 * sb).astype(jnp.bfloat16)
            sine = (s1 * cb + c1 * sb).astype(jnp.bfloat16)
            kmat[ch, 16 * a : 16 * a + 16, 0:BINS] = cosine
            kmat[ch, 16 * a : 16 * a + 16, BINS:] = -sine
            kmat[ch, BINS + 16 * a : BINS + 16 * a + 16, 0:BINS] = sine
            kmat[ch, BINS + 16 * a : BINS + 16 * a + 16, BINS:] = cosine

    time_a = (16 * col16).astype(jnp.float32) - 127.5
    time_b = (2 * (col16 % 8) + col16 // 8).astype(jnp.float32)
    scale = (g_f + 0.5) * (1.0 / (64 * 256))

    @pl.loop(0, CHUNKS)
    def _(ch):
        tile = jnp.where(ch < 4, first[0], first[1])
        rate = drift_v[pl.ds(4 * tile + ch % 4, 1), :] * scale
        ca, sa = cos_sin(time_a * rate)
        cb, sb = cos_sin(time_b * rate)
        for a in range(16):
            c1, s1 = ca[a : a + 1], sa[a : a + 1]
            cosine = c1 * cb - s1 * sb
            sine = s1 * cb + c1 * sb
            for s in range(2):
                at = s * N_TM + 8 * a
                rot_cos[ch, at : at + 8, :] = cosine[8 * s : 8 * s + 8]
                rot_sin[ch, at : at + 8, :] = sine[8 * s : 8 * s + 8]

    @pl.loop(0, N_ZH)
    def _(p):
        at = 8 * xy + 4 * (p % 2) + 2 * k
        t0 = table_s[2 * (p // 2) + 1, at]
        t1 = table_s[2 * (p // 2) + 1, at + 1]
        tiles = jnp.where(row8 < 4, t0, t1)
        for j in range(TILES_SUM):
            tile = 24 * (j // 3 * 2 + h) + 3 * z + j % 3
            masks[p, j] = jnp.where(tiles == tile, 1.0, 0.0)

    o, n = iota((256, 512), 0), iota((256, 512), 1)
    want = 4 * (o % N_TM) + 2 * (o // N_TM)
    perms = [
        jnp.where(n == want + c, 1.0, 0.0).astype(jnp.bfloat16) for c in range(2)
    ]

    pltpu.make_async_copy(
        recv2.at[pl.ds(0, N_TM - 1)], recv2.at[pl.ds(0, N_TM - 1)], s2_recv
    ).wait()

    got = recv2.reshape(4 * N_TM, BINS)[...]
    slab = jnp.concatenate(
        [jnp.dot(p, got, preferred_element_type=jnp.float32) for p in perms], axis=1
    ).astype(jnp.bfloat16)

    def stage3(r, tile):
        return pltpu.make_async_remote_copy(
            src_ref=part.at[tile], dst_ref=parts.at[zh, tile],
            send_sem=s3_send, recv_sem=s3_recv,
            device_id=zh_peer(r), device_id_type=MESH,
        )

    def send_tile(tile):
        @pl.loop(1, N_ZH)
        def _(r):
            stage3(r, tile).start()

    for ch in range(CHUNKS):
        product = jnp.dot(slab, kmat[ch], preferred_element_type=jnp.float32)
        turned = rot_cos[ch] * product[:, :BINS] - rot_sin[ch] * product[:, BINS:]
        part[ch // 4, ch % 4 : ch % 4 + 1, :] = jnp.sum(turned, axis=0, keepdims=True)
        if ch % 4 == 3:
            send_tile(ch // 4)

    parts[zh] = part[...]
    pltpu.make_async_copy(
        parts.at[pl.ds(0, N_ZH - 1)], parts.at[pl.ds(0, N_ZH - 1)], s3_recv
    ).wait()

    sums = [jnp.zeros((8, BINS), jnp.float32) for _ in range(TILES_SUM)]
    for p in range(N_ZH):
        terms = parts.reshape(N_ZH * 8, BINS)[8 * p : 8 * p + 8, :]
        for j in range(TILES_SUM):
            sums[j] += terms * masks[p, j]
    for j in range(TILES_SUM):
        at = 16 * (j // 3) + 4 * (j % 3)
        folded[at : at + 4, :] = sums[j][0:4] + sums[j][4:8]
    lane4 = iota((4, BINS), 1)
    for q in range(2):
        rows = [folded[pl.ds(16 * q + i, 4, stride=3), :] for i in range(3)]
        for j in range(4):
            at, shift = 96 * j // BINS, 96 * j % BINS
            low = pltpu.roll(rows[at], BINS - shift, 1) if shift else rows[at]
            if BINS - shift < PIX_OWN:
                high = pltpu.roll(rows[at + 1], BINS - shift, 1)
                low = jnp.where(lane4 < BINS - shift, low, high)
            for i in range(4):
                send4[(4 * i + j) * 2 + q] = low[i : i + 1]

    def stage4(r):
        return pltpu.make_async_remote_copy(
            src_ref=send4.at[rem(xyk + r, N_XYK)], dst_ref=recv4.at[xyk],
            send_sem=s4_send, recv_sem=s4_recv,
            device_id=xyk_peer(r), device_id_type=MESH,
        )

    @pl.loop(1, N_XYK)
    def _(r):
        stage4(r).start()

    recv4[xyk] = send4[xyk]
    hl.wait_send()
    for copy in sq_copies:
        copy.wait_send()
    pltpu.make_async_copy(
        send2.at[pl.ds(0, N_TM - 1)], send2.at[pl.ds(0, N_TM - 1)], s2_send
    ).wait()
    pltpu.make_async_copy(
        parts.at[pl.ds(0, N_ZH - 1)], parts.at[pl.ds(0, N_ZH - 1)], s3_send
    ).wait()
    pltpu.make_async_copy(
        send4.at[pl.ds(0, N_XYK - 1)], send4.at[pl.ds(0, N_XYK - 1)], s4_send
    ).wait()
    pltpu.make_async_copy(
        recv4.at[pl.ds(0, N_XYK - 1)], recv4.at[pl.ds(0, N_XYK - 1)], s4_recv
    ).wait()
    pieces = recv4.reshape(N_XYK, BINS)[...]
    total = jnp.sum(pieces, axis=0, keepdims=True)
    out_ref[...] = total * (1.0 / math.sqrt(256 * BINS))


def shards(spectra, valid, lags, drift, block_table):
    f32, bf16, i32 = jnp.float32, jnp.bfloat16, jnp.int32
    table = block_table.reshape(8, 128, 2).transpose(0, 2, 1).reshape(16, 128)
    dma = pltpu.SemaphoreType.DMA
    out = pl.pallas_call(
        kernel,
        out_shape=pltpu.VMEM((1, BINS), f32),
        in_specs=[pl.BlockSpec(memory_space=pltpu.HBM)] * 5,
        out_specs=pl.BlockSpec(memory_space=pltpu.VMEM),
        scratch_shapes=[
            pltpu.VMEM((128, BINS), bf16),
            pltpu.VMEM((128, BINS), bf16),
            pltpu.VMEM((384, 128), f32),
            pltpu.VMEM((384, 128), f32),
            pltpu.VMEM((16, 128), i32),
            pltpu.SMEM((16, 128), i32),
            pltpu.SMEM((2,), i32),
            pltpu.VMEM((8, BINS), f32),
            pltpu.VMEM((N_DET, 8, BINS), f32),
            pltpu.VMEM((N_TM, 4, BINS), bf16),
            pltpu.VMEM((N_TM, 4, BINS), bf16),
            pltpu.VMEM((CHUNKS, 256, 256), bf16),
            pltpu.VMEM((CHUNKS, 256, BINS), f32),
            pltpu.VMEM((CHUNKS, 256, BINS), f32),
            pltpu.VMEM((N_ZH, TILES_SUM, 8, BINS), f32),
            pltpu.VMEM((2, 4, BINS), f32),
            pltpu.VMEM((N_ZH, 2, 4, BINS), f32),
            pltpu.VMEM((32, BINS), f32),
            pltpu.VMEM((N_XYK, 1, BINS), f32),
            pltpu.VMEM((N_XYK, 1, BINS), f32),
            dma((6,)), dma, dma, dma((3,)), dma((3,)), dma, dma, dma, dma, dma, dma,
            pltpu.SemaphoreType.REGULAR, pltpu.SemaphoreType.REGULAR,
        ],
        compiler_params=pltpu.CompilerParams(
            collective_id=0, has_side_effects=True, vmem_limit_bytes=60 * 1024 * 1024
        ),
        name="radiometer",
    )(
        spectra.reshape(128, BINS),
        valid,
        lags.reshape(384, 128),
        drift.reshape(384, 128),
        table,
    )
    return out.reshape(BINS)[:PIX_OWN]


def solution(mesh):
    placed = (P("det", "tm", None, None, None), P("tm"), P(), P(), P())
    return jax.shard_map(
        shards, mesh=mesh, in_specs=placed, out_specs=P(("det", "tm")), check_vma=False
    )
```
